256 devices in a mesh: queue: 16 (over z, y_hi), space: 16 (over y_lo, x, core).
Axes of the slice: x: 4, y: 4 (y_hi: 2, y_lo: 2; y = y_hi * 2 + y_lo), z: 8, core: 2. Of those that a mesh axis runs over, the one named last changes fastest.
Arguments:
- latents: float32 [16, 128, 8, 64], P('queue', 'space'), may hold values from -6 to 6
- fresh_noise: float32 [1, 128, 64], P(None, 'space'), may hold values from -6 to 6
- levels: int32 [16, 8], replicated, may hold values from 0 to 999, as said below
- patch_weight: bfloat16 [64, 3072], replicated, may hold values from -0.75 to 0.75
- time_weight: bfloat16 [3072, 512], P(None, 'space'), may hold values from -0.109375 to 0.109375
- adaln_weight: bfloat16 [512, 6, 3072], P('space'), may hold values from -0.5 to 0.5
- qkv_weight: bfloat16 [3072, 3, 3072], P(None, None, 'space'), may hold values from -0.109375 to 0.109375
- out_weight: bfloat16 [3072, 3072], P('space'), may hold values from -0.75 to 0.75
- up_weight: bfloat16 [3072, 6144], P(None, 'space'), may hold values from -0.109375 to 0.109375
- down_weight: bfloat16 [6144, 3072], P('space'), may hold values from -0.21875 to 0.21875
- proj_weight: bfloat16 [3072, 64], replicated, may hold values from -0.109375 to 0.109375
Outputs:
- latents_out: float32 [16, 128, 8, 64], P('queue', 'space')
- predictions: float32 [1, 16, 128, 8, 64], P(None, 'queue', 'space')
The draws below stay inside these ranges and needn't reach their ends.
Inputs may be any that keep to these rules, and one draw needn't show every extreme that they name: levels fall strictly along the queue order q * 8 + f; the first is 999 and the last is 0.
All inputs are finite; a program needn't handle non-finite values.
Results may differ from the reference program's by a relative error of at most 0.03.
Values may be sent and summed in bfloat16 or wider, within the bound.
A program may use at most 128 MiB of HBM per device.

```python
import math
import jax
import jax.numpy as jnp
from jax import lax

D = 3072
HEADS = 48
HD = 64
TEMB = 512
P_SIZE = 64
FF = 6144
F = 8
STEPS = 1
NT = 1000
HW = 128
QSLOTS = 16
N_SPACE = 16


def draw_levels(key, part):
    key = jax.random.fold_in(key, 7)
    count = QSLOTS * F
    order = jax.random.permutation(key, NT - 2).astype(jnp.int32) + 1
    inner = -jnp.sort(-order[:count - 2])
    first = jnp.full((1,), NT - 1, jnp.int32)
    last = jnp.zeros((1,), jnp.int32)
    return jnp.concatenate([first, inner, last]).reshape(QSLOTS, F)


def block_scale(own_key, shape, cuts, smallest, largest):
    loudness = 1.0
    for position, shards_of in cuts:
        steps = jax.random.uniform(jax.random.fold_in(jax.random.fold_in(own_key, 6), position), (shards_of,), jnp.float32, smallest / len(cuts), largest / len(cuts))
        loudness = loudness * jnp.repeat(jnp.exp(steps), shape[position] // shards_of).reshape((-1,) + (1,) * (len(shape) - 1 - position))
    return loudness


def normal_values(rng, shape, deviation, bound, cuts=(), kind=jnp.bfloat16):
    level = block_scale(rng, shape, cuts, -0.22, 0.18) if cuts else 1.0
    array = jax.random.normal(rng, shape, jnp.float32) * deviation * level
    return jnp.minimum(jnp.maximum(array, -bound), bound).astype(kind)


def setup_inputs(seed: int = 0) -> dict:
    seeds = jax.random.split(jax.random.key(seed), 12)
    latents = normal_values(seeds[0], (QSLOTS, HW, F, P_SIZE), 1.0, 6.0, ((0, 16), (1, 16)), jnp.float32)
    fresh_noise = normal_values(seeds[1], (STEPS, HW, P_SIZE), 1.0, 6.0, ((1, 16),), jnp.float32)
    levels = draw_levels(jax.random.fold_in(seeds[11], 71), 0)
    patch_weight = normal_values(seeds[3], (P_SIZE, D), P_SIZE ** -0.5, 0.75)
    time_weight = normal_values(seeds[4], (D, TEMB), D ** -0.5, 0.109375, ((1, 16),))
    adaln_weight = normal_values(seeds[5], (TEMB, 6, D), (TEMB // 4) ** -0.5, 0.5, ((0, 16),))
    qkv_weight = normal_values(seeds[6], (D, 3, D), D ** -0.5, 0.109375, ((2, 16),))
    out_weight = normal_values(seeds[7], (D, D), HD ** -0.5, 0.75, ((0, 16),))
    up_weight = normal_values(seeds[8], (D, FF), D ** -0.5, 0.109375, ((1, 16),))
    down_weight = normal_values(seeds[9], (FF, D), (FF // 8) ** -0.5, 0.21875, ((0, 16),))
    proj_weight = normal_values(seeds[10], (D, P_SIZE), D ** -0.5, 0.109375)
    return {"latents": latents, "fresh_noise": fresh_noise, "levels": levels, "patch_weight": patch_weight, "time_weight": time_weight, "adaln_weight": adaln_weight, "qkv_weight": qkv_weight, "out_weight": out_weight, "up_weight": up_weight, "down_weight": down_weight, "proj_weight": proj_weight}


def noise_level(times):
    angle = (times / NT + 0.008) / 1.008 * (math.pi / 2)
    cosine = jnp.cos(angle)
    return 0.05 + 0.94 * cosine * cosine

def step_scales(levels):
    flat = levels.reshape(-1)
    later = jnp.concatenate([flat[1:], jnp.full((1,), -1, jnp.int32)])
    now = noise_level(flat.astype(jnp.float32))
    after = jnp.where(later < 0, jnp.float32(1.0), noise_level(later.astype(jnp.float32)))
    keep = jnp.sqrt(after / now)
    mix = jnp.sqrt(1.0 - after) - jnp.sqrt(after * (1.0 - now) / now)
    return (keep.reshape(levels.shape), mix.reshape(levels.shape))

def time_features(times, width):
    half = width // 2
    freqs = jnp.exp(-math.log(10000.0) * jnp.arange(half, dtype=jnp.float32) / half)
    angle = times.astype(jnp.float32)[:, None] * freqs[None, :]
    return jnp.concatenate([jnp.cos(angle), jnp.sin(angle)], -1)

def layer_norm(values, epsilon):
    centre = values - lax.optimization_barrier(jnp.mean(values, -1, keepdims=True))
    spread = lax.optimization_barrier(jnp.mean(centre * centre, -1, keepdims=True))
    return centre * lax.rsqrt(spread + epsilon)

def attention(projected, heads):
    total_rows = projected.shape[0]
    split = projected.reshape(total_rows, 3, heads, HD)
    queries = layer_norm(split[:, 0], 1e-06).astype(jnp.bfloat16)
    keys = layer_norm(split[:, 1], 1e-06).astype(jnp.bfloat16)
    values = split[:, 2].astype(jnp.bfloat16)
    scores = jnp.einsum('qhd,khd->hqk', queries.astype(jnp.float32), keys.astype(jnp.float32)) * HD ** (-0.5)
    weights = jnp.exp(scores)
    probs = (weights / lax.optimization_barrier(jnp.sum(weights, -1, keepdims=True))).astype(jnp.bfloat16)
    mixed = jnp.einsum('hqk,khd->qhd', probs.astype(jnp.float32), values.astype(jnp.float32))
    return mixed.astype(jnp.bfloat16).reshape(total_rows, heads * HD)

def group_sum(left, right):
    total_rows = left.shape[0]
    terms = jnp.einsum('tgc,gcd->gtd', left.reshape(total_rows, N_SPACE, -1).astype(jnp.float32), right.reshape(N_SPACE, -1, right.shape[1]).astype(jnp.float32))
    rounded = lax.optimization_barrier(terms.astype(jnp.bfloat16))
    return lax.optimization_barrier(jnp.sum(rounded.astype(jnp.float32), 0))

def slot_pass(latent, modulation, patch_weight, qkv_weight, out_weight, up_weight, down_weight, proj_weight):
    positions = latent.shape[0]
    total_rows = positions * F
    residual = jnp.dot(latent.astype(jnp.bfloat16).reshape(total_rows, P_SIZE), patch_weight, preferred_element_type=jnp.float32).reshape(positions, F, D)
    normed = (layer_norm(residual, 1e-05) * (1.0 + modulation[:, 1]) + modulation[:, 0]).astype(jnp.bfloat16)
    projected = jnp.dot(normed.reshape(total_rows, D), qkv_weight.reshape(D, 3 * D), preferred_element_type=jnp.float32)
    mixed = attention(projected, HEADS)
    attended = group_sum(mixed, out_weight).reshape(positions, F, D)
    residual = residual + modulation[:, 2] * attended
    normed = (layer_norm(residual, 1e-05) * (1.0 + modulation[:, 4]) + modulation[:, 3]).astype(jnp.bfloat16)
    hidden = jax.nn.gelu(jnp.dot(normed.reshape(total_rows, D), up_weight, preferred_element_type=jnp.float32), approximate=True).astype(jnp.bfloat16)
    fed = group_sum(hidden, down_weight).reshape(positions, F, D)
    residual = residual + modulation[:, 5] * fed
    final = layer_norm(residual, 1e-05).astype(jnp.bfloat16).reshape(total_rows, D)
    return jnp.dot(final, proj_weight, preferred_element_type=jnp.float32).reshape(positions, F, P_SIZE)

def reference(latents, fresh_noise, levels, patch_weight, time_weight, adaln_weight, qkv_weight, out_weight, up_weight, down_weight, proj_weight):
    keep, mix = step_scales(levels)
    features = time_features(levels.reshape(-1), D).astype(jnp.bfloat16)
    timing = jax.nn.silu(jnp.dot(features, time_weight, preferred_element_type=jnp.float32)).astype(jnp.bfloat16)
    modulation = jnp.dot(timing, adaln_weight.reshape(TEMB, 6 * D), preferred_element_type=jnp.float32).reshape(QSLOTS, F, 6, D)
    state = latents
    collected = []
    for turn in range(STEPS):
        predicted = lax.map(lambda pair: slot_pass(pair[0], pair[1], patch_weight, qkv_weight, out_weight, up_weight, down_weight, proj_weight), (state, modulation))
        moved = keep[:, None, :, None] * state + mix[:, None, :, None] * predicted
        carried = jnp.concatenate([fresh_noise[turn][None], moved[:-1, :, F - 1]], 0)
        state = jnp.concatenate([carried[:, :, None], moved[:, :, :F - 1]], 2)
        collected.append(predicted)
    return (state, jnp.stack(collected))
```

```python
import functools
import math

import jax
import jax.numpy as jnp
from jax import lax
from jax.experimental import pallas as pl
from jax.experimental.pallas import tpu as pltpu
from jax.sharding import PartitionSpec as P

MESH = pl.DeviceIdType.MESH
BF = jnp.bfloat16
F32 = jnp.float32
HD = 64
NT = 1000
NQ = 16
NS = 16
D = 3072
FR = 8
ROWS = 64
TOK = 1024
GROUP = 256
NC = 4
CW = D // NC
FS = 384
HS = 192
M1 = 2 * D // NS
M2 = 4 * D // NS


def noise_level(times):
    angle = (times / NT + 0.008) / 1.008 * (math.pi / 2)
    cosine = jnp.cos(angle)
    return 0.05 + 0.94 * cosine * cosine


def dot_nt(a, b):
    return lax.dot_general(a, b, (((1,), (1,)), ((), ())), preferred_element_type=F32)


def dot(a, b):
    return jnp.dot(a, b, preferred_element_type=F32)


def lnorm(v):
    centre = v - jnp.mean(v, -1, keepdims=True)
    spread = jnp.mean(centre * centre, -1, keepdims=True)
    return centre * lax.rsqrt(spread + 1e-05)


def kernel(
    lev, lat, noise, patch_h, tw_h, ada_h, qkv_h, out_h, up_h, down_h, proj_h,
    pred, lato,
    patch, tw, ada, qkv, proj, wo, wu, wd,
    p1, p2, rs1, rs2, mod1, mod2,
    xs, xb, xg, xet, acc_m, acc_s, abuf, mt, qt, kn, va, msend, mixt, mixa,
    res, own, s_o, s_r, s_l, p_r, p_l,
    rl1, rr1, ol1, or1, rl2, rr2, ol2, or2,
    nbuf, hacc, hid, mv, cs, cr,
    lsem, ps, pr, ys, yr, fs, fr, ms1, mr1, ms2, mr2, ms3, mr3, ms4, mr4, xss, xrs,
    as_, ar, ss1, sr1, ss2, sr2, gs, gr, csem,
):
    q = lax.axis_index("queue")
    s = lax.axis_index("space")
    core = lax.rem(s, 2)
    x = lax.rem(s // 2, 4)
    y = s // 8

    def at(y_, x_, c_):
        return (y_ * 4 + x_) * 2 + c_

    mate = at(y, x, 1 - core)
    over = at(1 - y, x, core)
    q_flip = q + 1 - 2 * lax.rem(q, 2)
    right = at(y, lax.rem(x + 1, 4), core)
    left = at(y, lax.rem(x + 3, 4), core)
    q_next = lax.rem(q + 1, NQ)
    q_prev = lax.rem(q + NQ - 1, NQ)

    def local(i, src, dst):
        return pltpu.make_async_copy(src, dst, lsem.at[i])

    def remote(src, dst, ssem, rsem, sp, qq=None):
        return pltpu.make_async_remote_copy(
            src_ref=src, dst_ref=dst, send_sem=ssem, recv_sem=rsem,
            device_id=(q if qq is None else qq, sp), device_id_type=MESH,
        )

    c_tw = local(0, tw_h, tw)
    c_ada = local(1, ada_h, ada)
    c_patch = local(2, patch_h, patch)
    c_qkv = local(3, qkv_h, qkv)
    c_wo = local(4, out_h, wo.at[pl.ds(0, HS)])
    c_wu = local(5, up_h, wu.at[:, pl.ds(0, FS)])
    c_wd = local(6, down_h, wd.at[pl.ds(0, FS)])
    c_proj = local(7, proj_h, proj)
    for c in (c_tw, c_ada, c_patch, c_qkv):
        c.start()

    bar = pltpu.get_barrier_semaphore()

    def hello(d, carry):
        pl.semaphore_signal(
            bar, inc=1, device_id=(q, lax.rem(s + d, NS)), device_id_type=MESH
        )
        return carry

    lax.fori_loop(1, NS, hello, 0)
    for dev in ((q_flip, over), (q_next, s), (q_prev, s)):
        pl.semaphore_signal(bar, inc=1, device_id=dev, device_id_type=MESH)

    row = lax.broadcasted_iota(jnp.int32, (FR, 128), 0)
    now = jnp.zeros((FR, 128), F32)
    later = jnp.zeros((FR, 128), F32)
    for f in range(FR):
        t_now = lev[f, q].astype(F32)
        if f < FR - 1:
            t_later = lev[f + 1, q].astype(F32)
        else:
            t_later = lev[0, jnp.minimum(q + 1, NQ - 1)].astype(F32)
        now = jnp.where(row == f, t_now, now)
        later = jnp.where(row == f, t_later, later)
    a_now = noise_level(now)
    a_after = noise_level(later)
    a_after = jnp.where((row == FR - 1) & (q == NQ - 1), 1.0, a_after)
    keep = jnp.sqrt(a_after / a_now)
    mix = jnp.sqrt(1.0 - a_after) - jnp.sqrt(a_after * (1.0 - a_now) / a_now)

    half = D // 2
    lane = lax.broadcasted_iota(jnp.int32, (FR, half), 1).astype(F32)
    freqs = jnp.exp(-math.log(10000.0) * lane / half)
    angle = now[:, 0:1] * freqs
    c_tw.wait()
    pre = dot_nt(jnp.cos(angle).astype(BF), tw[:, 0:half]) + dot_nt(
        jnp.sin(angle).astype(BF), tw[:, half:D]
    )
    timing = (pre * jax.nn.sigmoid(pre)).astype(BF)
    c_ada.wait()
    for k in range(2):
        p1[:, k * D : (k + 1) * D] = dot(timing, ada[k])

    c_patch.wait()
    x_own = lat[...]
    res[...] = dot(x_own.astype(BF), patch[...])
    full = res[...]
    centre = full - jnp.mean(full, -1, keepdims=True)
    spread = jnp.mean(centre * centre, -1, keepdims=True)
    rstd = lax.rsqrt(spread + 1e-05)
    r_hi = rstd.astype(BF).astype(F32)
    r_mid = (rstd - r_hi).astype(BF).astype(F32)
    r_lo = rstd - r_hi - r_mid
    xs[...] = jnp.zeros_like(xs)
    xs[:, 0:HD] = x_own
    lane_x = lax.broadcasted_iota(jnp.int32, (ROWS, 128), 1)
    packed = xs[...]
    packed = jnp.where(lane_x == 64, r_hi, packed)
    packed = jnp.where(lane_x == 65, r_mid, packed)
    packed = jnp.where(lane_x == 66, r_lo, packed)
    xb[...] = packed.astype(BF)

    def block(sp):
        return (lax.rem(sp, 2) + 2 * (sp // 8)) * 4 + lax.rem(sp // 2, 4)

    def xrows(sp):
        return pl.ds(pl.multiple_of(block(sp) * ROWS, ROWS), ROWS)

    xg[xrows(s), :] = xb[...]

    def cols(sp, width):
        return pl.ds(pl.multiple_of(sp * width, 128), width)

    pl.semaphore_wait(bar, NS + 2)

    def reduce_copy(part, recv, width, ssem, rsem, sp_to, sp_from, d):
        return remote(
            part.at[:, cols(sp_to, width)], recv.at[sp_from], ssem.at[d], rsem.at[sp_from], sp_to
        )

    def spread_copy(mod, width, ssem, rsem, sp_to, sp_from, d):
        view = mod.at[:, cols(sp_from, width)]
        return remote(view, view, ssem.at[d], rsem.at[sp_from], sp_to)

    def x_copy(sp_to, sp_from, d):
        return remote(xb, xg.at[xrows(sp_from), :], xss.at[d], xrs.at[sp_from], sp_to)

    def every(start):
        def step(d, carry):
            start(d, lax.rem(s + d, NS))
            return carry

        lax.fori_loop(1, NS, step, 0)

    every(lambda d, o: reduce_copy(p1, rs1, M1, ms1, mr1, o, s, d).start())
    every(lambda d, o: x_copy(o, s, d).start())

    w_wo = remote(out_h, wo.at[pl.ds(HS, HS)], ps.at[0], pr.at[0], mate)
    w_wu = remote(up_h, wu.at[:, pl.ds(FS, FS)], ps.at[1], pr.at[1], mate)
    w_wd = remote(down_h, wd.at[pl.ds(FS, FS)], ps.at[2], pr.at[2], mate)

    y_pairs = []
    f_copies = []

    def piece(i, source, target, forward_from, forward_to):
        pair = []
        for h, qq in ((0, None), (1, q_flip)):
            pair.append(remote(source(h), target(h), ys.at[i, h], yr.at[i, h], over, qq))
        y_pairs.append(pair)
        f_copies.append(remote(forward_from, forward_to, fs.at[i], fr.at[i], mate))

    ho = HS // 2
    piece(
        0,
        lambda h: out_h.at[pl.ds(h * ho, ho)],
        lambda h: wo.at[pl.ds(2 * HS + h * ho, ho)],
        wo.at[pl.ds(2 * HS, HS)],
        wo.at[pl.ds(3 * HS, HS)],
    )
    hu = CW // 2
    for k in range(NC):
        piece(
            1 + k,
            lambda h, k=k: up_h.at[pl.ds(k * CW + h * hu, hu)],
            lambda h, k=k: wu.at[pl.ds(k * CW + h * hu, hu), pl.ds(2 * FS, FS)],
            wu.at[pl.ds(k * CW, CW), pl.ds(2 * FS, FS)],
            wu.at[pl.ds(k * CW, CW), pl.ds(3 * FS, FS)],
        )
    hd = FS // 2
    for k in range(NC):
        piece(
            1 + NC + k,
            lambda h, k=k: down_h.at[pl.ds(h * hd, hd), pl.ds(k * CW, CW)],
            lambda h, k=k: wd.at[pl.ds(2 * FS + h * hd, hd), pl.ds(k * CW, CW)],
            wd.at[pl.ds(2 * FS, FS), pl.ds(k * CW, CW)],
            wd.at[pl.ds(3 * FS, FS), pl.ds(k * CW, CW)],
        )

    def push(i):
        for c in y_pairs[i]:
            c.start()

    def forward(i):
        for c in y_pairs[i]:
            c.wait_recv()
        f_copies[i].start()

    c_wo.start()
    w_wo.start()
    push(0)
    c_proj.start()

    for k in range(4):
        p2[:, k * D : (k + 1) * D] = dot(timing, ada[2 + k])
    every(lambda d, o: reduce_copy(p2, rs2, M2, ms2, mr2, o, s, d).start())

    def total(part, recv, mod, width, ssem, rsem):
        def add(d, acc):
            o = lax.rem(s + d, NS)
            reduce_copy(part, recv, width, ssem, rsem, s, o, d).wait_recv()
            return acc + recv[o]

        mod[:, cols(s, width)] = lax.fori_loop(1, NS, add, part[:, cols(s, width)])

    total(p1, rs1, mod1, M1, ms1, mr1)
    every(lambda d, o: spread_copy(mod1, M1, ms3, mr3, o, s, d).start())
    total(p2, rs2, mod2, M2, ms2, mr2)
    every(lambda d, o: spread_copy(mod2, M2, ms4, mr4, o, s, d).start())

    c_wu.start()
    w_wu.start()
    for k in range(NC):
        push(1 + k)

    every(lambda d, o: x_copy(s, o, d).wait_recv())
    xt = xg[...].astype(F32).T
    rstd_all = xt[64:65] + xt[65:66] + xt[66:67]
    frame = lax.rem(lax.broadcasted_iota(jnp.int32, (HD, TOK), 1), FR)
    xt = xt[0:HD]
    for f in range(FR):
        xet[f * HD : (f + 1) * HD, :] = jnp.where(frame == f, xt, 0.0).astype(BF)
    hot = (
        lax.rem(lax.broadcasted_iota(jnp.int32, (16, TOK), 1), FR)
        == lax.rem(lax.broadcasted_iota(jnp.int32, (16, TOK), 0), FR)
    ).astype(F32).astype(BF)

    every(lambda d, o: spread_copy(mod1, M1, ms3, mr3, s, o, d).wait_recv())
    c_qkv.wait()
    acc_m[...] = jnp.zeros_like(acc_m)
    acc_s[...] = jnp.zeros_like(acc_s)
    mean_w = jnp.mean(patch[...].astype(F32), -1, keepdims=True)

    def fold(j, carry):
        c = pl.ds(pl.multiple_of(j * CW, 128), CW)
        centred = patch[:, c].astype(F32) - mean_w
        gain = 1.0 + mod1[:, pl.ds(pl.multiple_of(D + j * CW, 128), CW)]
        for f in range(FR):
            abuf[f * HD : (f + 1) * HD, :] = (centred * gain[f : f + 1]).astype(BF)
        shift = mod1[:, c]
        hi = shift.astype(BF).astype(F32)
        both = jnp.concatenate([hi, shift - hi], 0).astype(BF)
        w = qkv[:, c]
        acc_m[...] += dot_nt(w, abuf[...])
        acc_s[...] += dot_nt(w, both)
        return carry

    lax.fori_loop(0, NC, fold, 0)
    mt[...] = acc_m[...].astype(BF)
    s_hi = acc_s[...].astype(BF)
    s_lo = (acc_s[...] - s_hi.astype(F32)).astype(BF)

    def project(k):
        r = slice(k * HS, (k + 1) * HS)
        out = dot(mt[r, :], xet[...]) * rstd_all
        return (out + dot(s_hi[r], hot) + dot(s_lo[r], hot)).reshape(3, HD, TOK)

    def head_norm(v):
        centre = v - jnp.mean(v, 1, keepdims=True)
        spread = jnp.mean(centre * centre, 1, keepdims=True)
        return centre * lax.rsqrt(spread + 1e-06)

    queries = head_norm(project(0)) * (HD**-0.5 / math.log(2.0))
    qt[...] = queries.astype(BF)
    keys = head_norm(project(1))
    for h in range(3):
        kn[h] = keys[h].T.astype(BF)
    values = project(2)
    for h in range(3):
        va[h, 0:HD, :] = values[h].astype(BF)
        va[h, HD : HD + 16, :] = jnp.ones((16, TOK), BF)

    def group_rows(slot):
        y_ = lax.rem(y + slot // 2, 2)
        c_ = lax.rem(core + slot, 2)
        return y_, c_

    def mix_copy(slot):
        y_, c_ = group_rows(slot)
        return remote(msend.at[slot], mixt.at[slot], as_.at[slot], ar.at[slot], at(y_, x, c_))

    def attend(i, carry):
        slot = 3 - i
        y_, c_ = group_rows(slot)
        g = pl.ds(pl.multiple_of((y_ * 2 + c_) * GROUP, GROUP), GROUP)
        for h in range(3):
            scores = dot(kn[h], qt[h, :, g])
            weights = jnp.exp2(scores).astype(BF)
            o = dot(va[h], weights)
            msend[slot, h * HD : (h + 1) * HD, :] = (o[0:HD] / o[HD : HD + 1]).astype(BF)

        @pl.when(slot > 0)
        def _():
            mix_copy(slot).start()

        return carry

    lax.fori_loop(0, 4, attend, 0)

    def turn(slot, src):
        v = src.astype(F32).T.astype(BF)
        for b in range(4):
            o = lax.rem(b - x + 4, 4)
            r = pl.ds(pl.multiple_of(o * ROWS, ROWS), ROWS)
            mixa[slot, r, :] = v[b * ROWS : (b + 1) * ROWS]

    turn(0, msend[0])
    forward(0)
    for slot in range(1, 4):
        mix_copy(slot).wait_recv()
        turn(slot, mixt[slot])
    c_wo.wait()
    w_wo.wait_recv()
    f_copies[0].wait_recv()

    def chunk(j):
        return pl.ds(pl.multiple_of(j * CW, 128), CW)

    lo, hi32 = pl.ds(0, 32), pl.ds(32, 32)

    def sum_phase(term, rl, rr, ol, or_, ss, sr):
        def sends(j):
            c = chunk(j)
            return dict(
                o_r=remote(s_o.at[lo, c], ol.at[:, c], ss.at[0, j], sr.at[0, j], right),
                o_l=remote(s_o.at[hi32, c], or_.at[:, c], ss.at[1, j], sr.at[1, j], left),
                d_r=remote(s_r.at[hi32, c], rl.at[hi32, c], ss.at[2, j], sr.at[2, j], right),
                d_l=remote(s_l.at[lo, c], rr.at[lo, c], ss.at[3, j], sr.at[3, j], left),
                a_r=remote(s_r.at[lo, c], rl.at[lo, c], ss.at[4, j], sr.at[4, j], right),
                a_l=remote(s_l.at[hi32, c], rr.at[hi32, c], ss.at[5, j], sr.at[5, j], left),
            )

        def passed(j):
            c = chunk(j)
            m = sends(j)
            m["o_r"].wait_recv()
            s_r[0:32, c] = (p_r[:, c] + ol[:, c].astype(F32)).astype(BF)
            m["a_r"].start()
            m["o_l"].wait_recv()
            s_l[32:64, c] = (p_l[:, c] + or_[:, c].astype(F32)).astype(BF)
            m["a_l"].start()

        def step(j, carry):
            c = chunk(j)
            v = term(c)
            m = sends(j)
            s_o[:, c] = v[128:192].astype(BF)
            m["o_r"].start()
            m["o_l"].start()
            s_r[32:64, c] = v[96:128].astype(BF)
            m["d_r"].start()
            s_l[0:32, c] = v[192:224].astype(BF)
            m["d_l"].start()
            p_r[:, c] = v[64:96]
            p_l[:, c] = v[224:256]
            own[:, c] = v[0:64]

            @pl.when(j > 0)
            def _():
                passed(j - 1)

            return carry

        lax.fori_loop(0, NC, step, 0)
        passed(NC - 1)

        def finish(j, carry):
            m = sends(j)
            for key in ("d_r", "d_l", "a_r", "a_l"):
                m[key].wait_recv()
            return carry

        lax.fori_loop(0, NC, finish, 0)

        def sent(j, carry):
            for c in sends(j).values():
                c.wait_send()
            return carry

        return lambda: lax.fori_loop(0, NC, sent, 0)

    def out_term(c):
        acc = dot(mixa[0], wo[0:HS, c])
        for slot in range(1, 4):
            acc += dot(mixa[slot], wo[slot * HS : (slot + 1) * HS, c])
        return acc

    sent1 = sum_phase(out_term, rl1, rr1, ol1, or1, ss1, sr1)

    c_wd.start()
    w_wd.start()
    for k in range(NC):
        push(1 + NC + k)

    every(lambda d, o: spread_copy(mod2, M2, ms4, mr4, s, o, d).wait_recv())

    def update(i, rl, rr, gate):
        r = pl.ds(pl.multiple_of(i * 16, 16), 16)
        summed = own[r, :] + rl[r, :].astype(F32) + rr[r, :].astype(F32)
        new = res[r, :].reshape(2, FR, D) + mod2[:, gate * D : (gate + 1) * D] * summed.reshape(2, FR, D)
        return r, new

    def second(i, carry):
        r, new = update(i, rl1, rr1, 0)
        res[r, :] = new.reshape(16, D)
        v = lnorm(new) * (1.0 + mod2[:, 2 * D : 3 * D]) + mod2[:, D : 2 * D]
        nbuf[r, :] = v.reshape(16, D).astype(BF)
        return carry

    lax.fori_loop(0, ROWS // 16, second, 0)

    def gathers(j):
        c = chunk(j)

        def go(i, src, dst, dev):
            return remote(
                nbuf.at[pl.ds(src, 32), c], nbuf.at[pl.ds(dst, 32), c], gs.at[i, j], gr.at[i, j], dev
            )

        return [
            go(0, 0, 192, right),
            go(1, 32, 96, left),
            go(2, 32, 224, right),
            go(3, 0, 64, left),
            go(4, 192, 128, right),
            go(5, 96, 160, left),
        ]

    def open_gather(j, carry):
        for c in gathers(j)[:4]:
            c.start()
        return carry

    lax.fori_loop(0, NC, open_gather, 0)

    def relay(j):
        m = gathers(j)
        m[0].wait_recv()
        m[4].start()
        m[1].wait_recv()
        m[5].start()

    hacc[...] = jnp.zeros_like(hacc)
    for k in range(NC):
        forward(1 + k)
    relay(0)
    c_wu.wait()
    w_wu.wait_recv()

    for j in range(NC):
        if j + 1 < NC:
            relay(j + 1)
        m = gathers(j)
        for i in range(2, 6):
            m[i].wait_recv()
        f_copies[1 + j].wait_recv()

        def widen(n, carry, j=j):
            c = pl.ds(pl.multiple_of(n * 512, 512), 512)
            hacc[:, c] += dot(nbuf[:, j * CW : (j + 1) * CW], wu[j * CW : (j + 1) * CW, c])
            return carry

        lax.fori_loop(0, 3, widen, 0)

    def activate(i, carry):
        r = pl.ds(pl.multiple_of(i * 16, 16), 16)
        hid[r, :] = jax.nn.gelu(hacc[r, :], approximate=True).astype(BF)
        return carry

    lax.fori_loop(0, GROUP // 16, activate, 0)
    for k in range(NC):
        forward(1 + NC + k)
    c_wd.wait()
    w_wd.wait_recv()
    for k in range(NC):
        f_copies[1 + NC + k].wait_recv()
    sent1()

    sent2 = sum_phase(lambda c: dot(hid[...], wd[:, c]), rl2, rr2, ol2, or2, ss2, sr2)

    def last(i, carry):
        r, new = update(i, rl2, rr2, 3)
        abuf_row = lnorm(new).reshape(16, D)
        for k in range(NC):
            s_o[r, k * CW : (k + 1) * CW] = abuf_row[:, k * CW : (k + 1) * CW].astype(BF)
        return carry

    sent2()
    lax.fori_loop(0, ROWS // 16, last, 0)
    c_proj.wait()
    out = dot_nt(s_o[...], proj[...])
    pred[...] = out
    moved = keep[:, 0:HD] * lat[...].reshape(FR, FR, HD) + mix[:, 0:HD] * out.reshape(FR, FR, HD)
    mv[...] = jnp.zeros_like(mv)
    mv[:, 0:HD] = moved.reshape(ROWS, HD)
    cs[...] = mv[pl.ds(FR - 1, FR, stride=FR), :]
    carry_copy = remote(cs, cr, csem.at[0], csem.at[1], s, q_next)
    carry_copy.start()
    for f in range(1, FR):
        lato[pl.ds(f, FR, stride=FR), :] = mv[pl.ds(f - 1, FR, stride=FR), :][:, 0:HD]

    every(lambda d, o: reduce_copy(p1, rs1, M1, ms1, mr1, o, s, d).wait_send())
    every(lambda d, o: reduce_copy(p2, rs2, M2, ms2, mr2, o, s, d).wait_send())
    every(lambda d, o: spread_copy(mod1, M1, ms3, mr3, o, s, d).wait_send())
    every(lambda d, o: spread_copy(mod2, M2, ms4, mr4, o, s, d).wait_send())
    every(lambda d, o: x_copy(o, s, d).wait_send())
    for slot in range(1, 4):
        mix_copy(slot).wait_send()
    for c in (w_wo, w_wu, w_wd):
        c.wait_send()
    for pair in y_pairs:
        for c in pair:
            c.wait_send()
    for c in f_copies:
        c.wait_send()

    def gathered(j, carry):
        for c in gathers(j):
            c.wait_send()
        return carry

    lax.fori_loop(0, NC, gathered, 0)
    carry_copy.wait()
    lato[pl.ds(0, FR, stride=FR), :] = jnp.where(q == 0, noise[...], cr[:, 0:HD])


def scratch():
    v = pltpu.VMEM
    dma = pltpu.SemaphoreType.DMA
    return [
        v((HD, D), BF), v((32, D), BF), v((6, 32, D), BF), v((3 * HS, D), BF), v((HD, D), BF),
        v((4 * HS, D), BF), v((D, 4 * FS), BF), v((4 * FS, D), BF),
        v((FR, 2 * D), F32), v((FR, 4 * D), F32), v((NS, FR, M1), F32), v((NS, FR, M2), F32),
        v((FR, 2 * D), F32), v((FR, 4 * D), F32),
        v((ROWS, 128), F32), v((ROWS, 128), BF), v((TOK, 128), BF), v((FR * HD, TOK), BF),
        v((3 * HS, FR * HD), F32), v((3 * HS, 16), F32), v((FR * HD, CW), BF),
        v((3 * HS, FR * HD), BF),
        v((3, HD, TOK), BF), v((3, TOK, HD), BF), v((3, HD + 16, TOK), BF),
        v((4, HS, GROUP), BF), v((4, HS, GROUP), BF), v((4, GROUP, HS), BF),
        v((ROWS, D), F32), v((ROWS, D), F32), v((ROWS, D), BF), v((ROWS, D), BF), v((ROWS, D), BF),
        v((32, D), F32), v((32, D), F32),
        v((ROWS, D), BF), v((ROWS, D), BF), v((32, D), BF), v((32, D), BF),
        v((ROWS, D), BF), v((ROWS, D), BF), v((32, D), BF), v((32, D), BF),
        v((GROUP, D), BF), v((GROUP, 4 * FS), F32), v((GROUP, 4 * FS), BF),
        v((ROWS, 128), F32), v((FR, 128), F32), v((FR, 128), F32),
        dma((8,)), dma((3,)), dma((3,)), dma((9, 2)), dma((9, 2)), dma((9,)), dma((9,)),
        dma((NS,)), dma((NS,)), dma((NS,)), dma((NS,)), dma((NS,)), dma((NS,)), dma((NS,)), dma((NS,)),
        dma((NS,)), dma((NS,)),
        dma((4,)), dma((4,)),
        dma((6, NC)), dma((6, NC)), dma((6, NC)), dma((6, NC)), dma((6, NC)), dma((6, NC)),
        dma((2,)),
    ]


def body(
    latents, fresh_noise, levels, patch_weight, time_weight, adaln_weight, qkv_weight,
    out_weight, up_weight, down_weight, proj_weight,
):
    vm = pl.BlockSpec(memory_space=pltpu.VMEM)
    hbm = pl.BlockSpec(memory_space=pl.ANY)
    pred, lato = pl.pallas_call(
        kernel,
        out_shape=(
            jax.ShapeDtypeStruct((ROWS, HD), F32),
            jax.ShapeDtypeStruct((ROWS, HD), F32),
        ),
        in_specs=[pl.BlockSpec(memory_space=pltpu.SMEM), vm, vm] + [hbm] * 8,
        out_specs=(vm, vm),
        scratch_shapes=scratch(),
        compiler_params=pltpu.CompilerParams(
            collective_id=0, has_side_effects=True, vmem_limit_bytes=60 * 1024 * 1024
        ),
    )(
        levels.T,
        latents.reshape(ROWS, HD),
        fresh_noise.reshape(FR, HD),
        patch_weight,
        time_weight.T,
        jnp.transpose(adaln_weight, (1, 0, 2)),
        jnp.transpose(qkv_weight, (1, 2, 0)).reshape(3 * HS, D),
        out_weight,
        up_weight,
        down_weight,
        proj_weight.T,
    )
    return lato.reshape(1, 8, FR, HD), pred.reshape(1, 1, 8, FR, HD)


def solution(mesh):
    in_specs = (
        P("queue", "space", None, None),
        P(None, "space", None),
        P(),
        P(),
        P(None, "space"),
        P("space", None, None),
        P(None, None, "space"),
        P("space", None),
        P(None, "space"),
        P("space", None),
        P(),
    )
    out_specs = (P("queue", "space", None, None), P(None, "queue", "space", None, None))
    return jax.shard_map(body, mesh=mesh, in_specs=in_specs, out_specs=out_specs, check_vma=False)
```

```python
import functools
import math

import jax
import jax.numpy as jnp
from jax import lax
from jax.experimental import pallas as pl
from jax.experimental.pallas import tpu as pltpu
from jax.sharding import PartitionSpec as P

MESH = pl.DeviceIdType.MESH
BF = jnp.bfloat16
F32 = jnp.float32
HD = 64
NT = 1000
NQ = 16
NS = 16
D = 3072
FR = 8
ROWS = 64
TOK = 1024
GROUP = 256
NC = 4
CW = D // NC
FS = 384
HS = 192
M1 = 2 * D // 8
M2 = 4 * D // 8


def noise_level(times):
    angle = (times / NT + 0.008) / 1.008 * (math.pi / 2)
    cosine = jnp.cos(angle)
    return 0.05 + 0.94 * cosine * cosine


def dot_nt(a, b):
    return lax.dot_general(a, b, (((1,), (1,)), ((), ())), preferred_element_type=F32)


def dot(a, b):
    return jnp.dot(a, b, preferred_element_type=F32)


def lnorm(v):
    centre = v - jnp.mean(v, -1, keepdims=True)
    spread = jnp.mean(centre * centre, -1, keepdims=True)
    return centre * lax.rsqrt(spread + 1e-05)


def kernel(
    lev, lat, noise, patch_h, tw_h, ada_h, qkv_h, out_h, up_h, down_h, proj_h,
    pred, lato,
    patch, tw, ada, qkv, proj, wo, wu, wd,
    p1, p2, ra1, ra2, rb1, rb2, b1, b2, t1, t2, mod1, mod2,
    xs, xg, xet, acc_m, acc_s, abuf, mt, qt, kn, va, msend, mixt, mixa,
    res, own, s_o, s_r, s_l, p_r, p_l,
    rl1, rr1, ol1, or1, rl2, rr2, ol2, or2,
    nbuf, hacc, hid, mv, cs, cr,
    lsem, ps, pr, ys, yr, zs, zr, fs, fr, mss, msr, xss, xrs,
    as_, ar, ss1, sr1, ss2, sr2, gs, gr, csem,
):
    q = lax.axis_index("queue")
    s = lax.axis_index("space")
    core = lax.rem(s, 2)
    x = lax.rem(s // 2, 4)
    y = s // 8

    def at(y_, x_, c_):
        return (y_ * 4 + x_) * 2 + c_

    mate = at(y, x, 1 - core)
    over = at(1 - y, x, core)
    q_flip = q + 1 - 2 * lax.rem(q, 2)
    right = at(y, lax.rem(x + 1, 4), core)
    left = at(y, lax.rem(x + 3, 4), core)
    q_next = lax.rem(q + 1, NQ)
    q_prev = lax.rem(q + NQ - 1, NQ)

    def local(i, src, dst):
        return pltpu.make_async_copy(src, dst, lsem.at[i])

    def remote(src, dst, ssem, rsem, sp, qq=None):
        return pltpu.make_async_remote_copy(
            src_ref=src, dst_ref=dst, send_sem=ssem, recv_sem=rsem,
            device_id=(q if qq is None else qq, sp), device_id_type=MESH,
        )

    c_tw = local(0, tw_h, tw)
    c_ada = local(1, ada_h, ada)
    c_patch = local(2, patch_h, patch)
    c_qkv = local(3, qkv_h, qkv)
    c_wo = local(4, out_h, wo.at[pl.ds(0, HS)])
    c_wu = local(5, up_h, wu.at[:, pl.ds(0, FS)])
    c_wd = local(6, down_h, wd.at[pl.ds(0, FS)])
    c_proj = local(7, proj_h, proj)
    for c in (c_tw, c_ada, c_patch, c_qkv):
        c.start()

    bar = pltpu.get_barrier_semaphore()

    group = ((mate, 1), (over, 2), (at(1 - y, x, 1 - core), 3))
    ring = ((right, 1), (at(y, lax.rem(x + 2, 4), core), 2), (left, 3))
    par = lax.rem(q // 2, 2)
    z_to = [lax.rem(q + NQ + 2 * (1 - 2 * par) * (1 - 2 * h), NQ) for h in range(2)]
    for dev in (
        [(q, o) for o, _ in group + ring]
        + [(q_flip, over), (q_next, s), (q_prev, s), (z_to[0], s), (z_to[1], s)]
    ):
        pl.semaphore_signal(bar, inc=1, device_id=dev, device_id_type=MESH)

    row = lax.broadcasted_iota(jnp.int32, (FR, 128), 0)
    now = jnp.zeros((FR, 128), F32)
    later = jnp.zeros((FR, 128), F32)
    for f in range(FR):
        t_now = lev[f, q].astype(F32)
        if f < FR - 1:
            t_later = lev[f + 1, q].astype(F32)
        else:
            t_later = lev[0, jnp.minimum(q + 1, NQ - 1)].astype(F32)
        now = jnp.where(row == f, t_now, now)
        later = jnp.where(row == f, t_later, later)
    a_now = noise_level(now)
    a_after = noise_level(later)
    a_after = jnp.where((row == FR - 1) & (q == NQ - 1), 1.0, a_after)
    keep = jnp.sqrt(a_after / a_now)
    mix = jnp.sqrt(1.0 - a_after) - jnp.sqrt(a_after * (1.0 - a_now) / a_now)

    half = D // 2
    lane = lax.broadcasted_iota(jnp.int32, (FR, half), 1).astype(F32)
    freqs = jnp.exp(-math.log(10000.0) * lane / half)
    angle = now[:, 0:1] * freqs
    c_tw.wait()
    pre = dot_nt(jnp.cos(angle).astype(BF), tw[:, 0:half]) + dot_nt(
        jnp.sin(angle).astype(BF), tw[:, half:D]
    )
    timing = (pre * jax.nn.sigmoid(pre)).astype(BF)
    c_ada.wait()
    for k in range(2):
        part = dot(timing, ada[k])
        for h in range(2):
            two = [part[:, (2 * h + i) * M1 : (2 * h + i + 1) * M1] for i in range(2)]
            p1[2 * k + h] = jnp.concatenate(two, 0).astype(BF)

    c_patch.wait()
    x_own = lat[...]
    res[...] = dot(x_own.astype(BF), patch[...])
    full = res[...]
    centre = full - jnp.mean(full, -1, keepdims=True)
    spread = jnp.mean(centre * centre, -1, keepdims=True)
    rstd = lax.rsqrt(spread + 1e-05)
    r_hi = rstd.astype(BF).astype(F32)
    r_mid = (rstd - r_hi).astype(BF).astype(F32)
    r_lo = rstd - r_hi - r_mid
    xs[...] = jnp.zeros_like(xs)
    xs[:, 0:HD] = x_own
    lane_x = lax.broadcasted_iota(jnp.int32, (ROWS, 128), 1)
    packed = xs[...]
    packed = jnp.where(lane_x == 64, r_hi, packed)
    packed = jnp.where(lane_x == 65, r_mid, packed)
    packed = jnp.where(lane_x == 66, r_lo, packed)
    me4 = y * 2 + core
    xg[x, me4] = packed.astype(BF)

    pl.semaphore_wait(bar, 11)

    def slot_of(slot):
        return lax.rem(y + slot // 2, 2) * 2 + lax.rem(core + slot, 2)

    def group_sum(k, part, recv):
        ssem, rsem = mss.at[0, k], msr.at[0, k]
        return [
            remote(part.at[slot_of(i)], recv.at[i], ssem.at[i], rsem.at[i], o) for o, i in group
        ]

    def ring_sum(k, mine, recv):
        ssem, rsem = mss.at[1, k], msr.at[1, k]
        return [remote(mine, recv.at[i], ssem.at[i], rsem.at[i], o) for o, i in ring]

    def group_spread(k, tot):
        ssem, rsem = mss.at[2, k], msr.at[2, k]
        return [
            remote(tot.at[me4], tot.at[me4], ssem.at[i], rsem.at[i], o) for o, i in group
        ]

    x_near = [
        remote(xg.at[x, me4], xg.at[x, me4], xss.at[0, i], xrs.at[0, i], o) for o, i in group
    ]
    x_far = [remote(xg.at[x], xg.at[x], xss.at[1, i], xrs.at[1, i], o) for o, i in ring]

    def begin(copies):
        for c in copies:
            c.start()

    def arrive(copies):
        for c in copies:
            c.wait_recv()

    steps = []
    for k, (part, ra, mine, rb, tot) in enumerate(((p1, ra1, b1, rb1, t1), (p2, ra2, b2, rb2, t2))):
        steps.append((group_sum(k, part, ra), ring_sum(k, mine, rb), group_spread(k, tot)))

    def join(k):
        part, ra, mine = ((p1, ra1, b1), (p2, ra2, b2))[k]
        arrive(steps[k][0])
        acc = part[me4].astype(F32)
        for i in range(1, 4):
            acc += ra[i].astype(F32)
        mine[...] = acc.astype(BF)
        begin(steps[k][1])

    def close(k):
        mine, rb, tot = ((b1, rb1, t1), (b2, rb2, t2))[k]
        arrive(steps[k][1])
        acc = mine[...].astype(F32)
        for i in range(1, 4):
            acc += rb[i].astype(F32)
        tot[me4] = acc.astype(BF)
        begin(steps[k][2])

    def unpack(k):
        tot, mod, w = ((t1, mod1, M1), (t2, mod2, M2))[k]
        arrive(steps[k][2])
        for m in range(4):
            v = tot[m].astype(F32)
            mod[:, 2 * m * w : (2 * m + 1) * w] = v[0:FR]
            mod[:, (2 * m + 1) * w : (2 * m + 2) * w] = v[FR : 2 * FR]

    begin(steps[0][0])
    begin(x_near)

    w_wo = remote(out_h, wo.at[pl.ds(HS, HS)], ps.at[0], pr.at[0], mate)
    w_wu = remote(up_h, wu.at[:, pl.ds(FS, FS)], ps.at[1], pr.at[1], mate)
    w_wd = remote(down_h, wd.at[pl.ds(FS, FS)], ps.at[2], pr.at[2], mate)

    y_pairs = []
    z_sends = []
    z_recvs = []
    f_copies = []

    def piece(i, source, target, forward_from, forward_to):
        mine = [2 * par + h for h in range(2)]
        theirs = [2 * (1 - par) + h for h in range(2)]
        y_pairs.append([
            remote(source(mine[h]), target(mine[h]), ys.at[i, h], yr.at[i, h], over, (q, q_flip)[h])
            for h in range(2)
        ])
        for lst, parts in ((z_sends, mine), (z_recvs, theirs)):
            lst.append([
                remote(target(parts[h]), target(parts[h]), zs.at[i, h], zr.at[i, h], s, z_to[h])
                for h in range(2)
            ])
        f_copies.append(remote(forward_from, forward_to, fs.at[i], fr.at[i], mate))

    def rows_of(base, part, size):
        return pl.ds(pl.multiple_of(base + part * size, 16), size)

    piece(
        0,
        lambda p: out_h.at[rows_of(0, p, HS // 4)],
        lambda p: wo.at[rows_of(2 * HS, p, HS // 4)],
        wo.at[pl.ds(2 * HS, HS)],
        wo.at[pl.ds(3 * HS, HS)],
    )
    for k in range(NC):
        piece(
            1 + k,
            lambda p, k=k: up_h.at[rows_of(k * CW, p, CW // 4)],
            lambda p, k=k: wu.at[rows_of(k * CW, p, CW // 4), pl.ds(2 * FS, FS)],
            wu.at[pl.ds(k * CW, CW), pl.ds(2 * FS, FS)],
            wu.at[pl.ds(k * CW, CW), pl.ds(3 * FS, FS)],
        )
    for k in range(NC):
        piece(
            1 + NC + k,
            lambda p, k=k: down_h.at[rows_of(0, p, FS // 4), pl.ds(k * CW, CW)],
            lambda p, k=k: wd.at[rows_of(2 * FS, p, FS // 4), pl.ds(k * CW, CW)],
            wd.at[pl.ds(2 * FS, FS), pl.ds(k * CW, CW)],
            wd.at[pl.ds(3 * FS, FS), pl.ds(k * CW, CW)],
        )

    def push(i):
        begin(y_pairs[i])

    def along(i):
        arrive(y_pairs[i])
        begin(z_sends[i])

    def forward(i):
        arrive(z_recvs[i])
        f_copies[i].start()

    c_wo.start()
    w_wo.start()
    c_proj.start()

    for k in range(4):
        part = dot(timing, ada[2 + k])
        p2[k] = jnp.concatenate([part[:, 0:M2], part[:, M2 : 2 * M2]], 0).astype(BF)
    begin(steps[1][0])
    join(0)
    arrive(x_near)
    begin(x_far)
    join(1)
    close(0)
    push(0)
    close(1)
    c_wu.start()
    w_wu.start()
    push(1)
    push(2)

    arrive(x_far)
    xt = jnp.concatenate([xg[b, m] for m in range(4) for b in range(4)], 0).astype(F32).T
    rstd_all = xt[64:65] + xt[65:66] + xt[66:67]
    frame = lax.rem(lax.broadcasted_iota(jnp.int32, (HD, TOK), 1), FR)
    xt = xt[0:HD]
    for f in range(FR):
        xet[f * HD : (f + 1) * HD, :] = jnp.where(frame == f, xt, 0.0).astype(BF)
    hot = (
        lax.rem(lax.broadcasted_iota(jnp.int32, (16, TOK), 1), FR)
        == lax.rem(lax.broadcasted_iota(jnp.int32, (16, TOK), 0), FR)
    ).astype(F32).astype(BF)

    unpack(0)
    c_qkv.wait()
    acc_m[...] = jnp.zeros_like(acc_m)
    acc_s[...] = jnp.zeros_like(acc_s)
    mean_w = jnp.mean(patch[...].astype(F32), -1, keepdims=True)

    def fold(j, carry):
        c = pl.ds(pl.multiple_of(j * CW, 128), CW)
        centred = patch[:, c].astype(F32) - mean_w
        gain = 1.0 + mod1[:, pl.ds(pl.multiple_of(D + j * CW, 128), CW)]
        for f in range(FR):
            abuf[f * HD : (f + 1) * HD, :] = (centred * gain[f : f + 1]).astype(BF)
        shift = mod1[:, c]
        hi = shift.astype(BF).astype(F32)
        both = jnp.concatenate([hi, shift - hi], 0).astype(BF)
        w = qkv[:, c]
        acc_m[...] += dot_nt(w, abuf[...])
        acc_s[...] += dot_nt(w, both)
        return carry

    lax.fori_loop(0, NC, fold, 0)
    along(0)
    push(3)
    push(4)
    mt[...] = acc_m[...].astype(BF)
    s_hi = acc_s[...].astype(BF)
    s_lo = (acc_s[...] - s_hi.astype(F32)).astype(BF)

    def project(k):
        r = slice(k * HS, (k + 1) * HS)
        out = dot(mt[r, :], xet[...]) * rstd_all
        return (out + dot(s_hi[r], hot) + dot(s_lo[r], hot)).reshape(3, HD, TOK)

    def head_norm(v):
        centre = v - jnp.mean(v, 1, keepdims=True)
        spread = jnp.mean(centre * centre, 1, keepdims=True)
        return centre * lax.rsqrt(spread + 1e-06)

    queries = head_norm(project(0)) * (HD**-0.5 / math.log(2.0))
    qt[...] = queries.astype(BF)
    keys = head_norm(project(1))
    for h in range(3):
        kn[h] = keys[h].T.astype(BF)
    values = project(2)
    for h in range(3):
        va[h, 0:HD, :] = values[h].astype(BF)
        va[h, HD : HD + 16, :] = jnp.ones((16, TOK), BF)

    along(1)
    along(2)

    def group_rows(slot):
        y_ = lax.rem(y + slot // 2, 2)
        c_ = lax.rem(core + slot, 2)
        return y_, c_

    def mix_copy(slot):
        y_, c_ = group_rows(slot)
        return remote(msend.at[slot], mixt.at[slot], as_.at[slot], ar.at[slot], at(y_, x, c_))

    def attend(i, carry):
        slot = 3 - i
        y_, c_ = group_rows(slot)
        g = pl.ds(pl.multiple_of((y_ * 2 + c_) * GROUP, GROUP), GROUP)
        for h in range(3):
            scores = dot(kn[h], qt[h, :, g])
            weights = jnp.exp2(scores).astype(BF)
            o = dot(va[h], weights)
            msend[slot, h * HD : (h + 1) * HD, :] = (o[0:HD] / o[HD : HD + 1]).astype(BF)

        @pl.when(slot > 0)
        def _():
            mix_copy(slot).start()

        return carry

    lax.fori_loop(0, 4, attend, 0)

    def turn(slot, src):
        v = src.astype(F32).T.astype(BF)
        for b in range(4):
            o = lax.rem(b - x + 4, 4)
            r = pl.ds(pl.multiple_of(o * ROWS, ROWS), ROWS)
            mixa[slot, r, :] = v[b * ROWS : (b + 1) * ROWS]

    turn(0, msend[0])
    forward(0)
    for slot in range(1, 4):
        mix_copy(slot).wait_recv()
        turn(slot, mixt[slot])
    c_wd.start()
    w_wd.start()
    for k in range(NC):
        push(1 + NC + k)
    along(3)
    along(4)
    c_wo.wait()
    w_wo.wait_recv()
    f_copies[0].wait_recv()

    def chunk(j):
        return pl.ds(pl.multiple_of(j * CW, 128), CW)

    lo, hi32 = pl.ds(0, 32), pl.ds(32, 32)

    def sum_phase(term, rl, rr, ol, or_, ss, sr):
        def sends(j):
            c = chunk(j)
            return dict(
                o_r=remote(s_o.at[lo, c], ol.at[:, c], ss.at[0, j], sr.at[0, j], right),
                o_l=remote(s_o.at[hi32, c], or_.at[:, c], ss.at[1, j], sr.at[1, j], left),
                d_r=remote(s_r.at[hi32, c], rl.at[hi32, c], ss.at[2, j], sr.at[2, j], right),
                d_l=remote(s_l.at[lo, c], rr.at[lo, c], ss.at[3, j], sr.at[3, j], left),
                a_r=remote(s_r.at[lo, c], rl.at[lo, c], ss.at[4, j], sr.at[4, j], right),
                a_l=remote(s_l.at[hi32, c], rr.at[hi32, c], ss.at[5, j], sr.at[5, j], left),
            )

        def passed(j):
            c = chunk(j)
            m = sends(j)
            m["o_r"].wait_recv()
            s_r[0:32, c] = (p_r[:, c] + ol[:, c].astype(F32)).astype(BF)
            m["a_r"].start()
            m["o_l"].wait_recv()
            s_l[32:64, c] = (p_l[:, c] + or_[:, c].astype(F32)).astype(BF)
            m["a_l"].start()

        def step(j, carry):
            c = chunk(j)
            v = term(c)
            m = sends(j)
            s_o[:, c] = v[128:192].astype(BF)
            m["o_r"].start()
            m["o_l"].start()
            s_r[32:64, c] = v[96:128].astype(BF)
            m["d_r"].start()
            s_l[0:32, c] = v[192:224].astype(BF)
            m["d_l"].start()
            p_r[:, c] = v[64:96]
            p_l[:, c] = v[224:256]
            own[:, c] = v[0:64]

            @pl.when(j > 0)
            def _():
                passed(j - 1)

            return carry

        lax.fori_loop(0, NC, step, 0)
        passed(NC - 1)

        def finish(j, carry):
            m = sends(j)
            for key in ("d_r", "d_l", "a_r", "a_l"):
                m[key].wait_recv()
            return carry

        lax.fori_loop(0, NC, finish, 0)

        def sent(j, carry):
            for c in sends(j).values():
                c.wait_send()
            return carry

        return lambda: lax.fori_loop(0, NC, sent, 0)

    def out_term(c):
        acc = dot(mixa[0], wo[0:HS, c])
        for slot in range(1, 4):
            acc += dot(mixa[slot], wo[slot * HS : (slot + 1) * HS, c])
        return acc

    sent1 = sum_phase(out_term, rl1, rr1, ol1, or1, ss1, sr1)


    unpack(1)

    def update(i, rl, rr, gate):
        r = pl.ds(pl.multiple_of(i * 16, 16), 16)
        summed = own[r, :] + rl[r, :].astype(F32) + rr[r, :].astype(F32)
        new = res[r, :].reshape(2, FR, D) + mod2[:, gate * D : (gate + 1) * D] * summed.reshape(2, FR, D)
        return r, new

    def second(i, carry):
        r, new = update(i, rl1, rr1, 0)
        res[r, :] = new.reshape(16, D)
        v = lnorm(new) * (1.0 + mod2[:, 2 * D : 3 * D]) + mod2[:, D : 2 * D]
        nbuf[r, :] = v.reshape(16, D).astype(BF)
        return carry

    lax.fori_loop(0, ROWS // 16, second, 0)

    def gathers(j):
        c = chunk(j)

        def go(i, src, dst, dev):
            return remote(
                nbuf.at[pl.ds(src, 32), c], nbuf.at[pl.ds(dst, 32), c], gs.at[i, j], gr.at[i, j], dev
            )

        return [
            go(0, 0, 192, right),
            go(1, 32, 96, left),
            go(2, 32, 224, right),
            go(3, 0, 64, left),
            go(4, 192, 128, right),
            go(5, 96, 160, left),
        ]

    def open_gather(j, carry):
        for c in gathers(j)[:4]:
            c.start()
        return carry

    lax.fori_loop(0, NC, open_gather, 0)

    def relay(j):
        m = gathers(j)
        m[0].wait_recv()
        m[4].start()
        m[1].wait_recv()
        m[5].start()

    hacc[...] = jnp.zeros_like(hacc)
    for k in range(NC):
        forward(1 + k)
        along(1 + NC + k)
    relay(0)
    c_wu.wait()
    w_wu.wait_recv()

    for j in range(NC):
        if j + 1 < NC:
            relay(j + 1)
        m = gathers(j)
        for i in range(2, 6):
            m[i].wait_recv()
        f_copies[1 + j].wait_recv()

        def widen(n, carry, j=j):
            c = pl.ds(pl.multiple_of(n * 512, 512), 512)
            hacc[:, c] += dot(nbuf[:, j * CW : (j + 1) * CW], wu[j * CW : (j + 1) * CW, c])
            return carry

        lax.fori_loop(0, 3, widen, 0)

    def activate(i, carry):
        r = pl.ds(pl.multiple_of(i * 16, 16), 16)
        hid[r, :] = jax.nn.gelu(hacc[r, :], approximate=True).astype(BF)
        return carry

    lax.fori_loop(0, GROUP // 16, activate, 0)
    for k in range(NC):
        forward(1 + NC + k)
    c_wd.wait()
    w_wd.wait_recv()
    for k in range(NC):
        f_copies[1 + NC + k].wait_recv()
    sent1()

    sent2 = sum_phase(lambda c: dot(hid[...], wd[:, c]), rl2, rr2, ol2, or2, ss2, sr2)

    def last(i, carry):
        r, new = update(i, rl2, rr2, 3)
        abuf_row = lnorm(new).reshape(16, D)
        for k in range(NC):
            s_o[r, k * CW : (k + 1) * CW] = abuf_row[:, k * CW : (k + 1) * CW].astype(BF)
        return carry

    sent2()
    lax.fori_loop(0, ROWS // 16, last, 0)
    c_proj.wait()
    out = dot_nt(s_o[...], proj[...])
    pred[...] = out
    moved = keep[:, 0:HD] * lat[...].reshape(FR, FR, HD) + mix[:, 0:HD] * out.reshape(FR, FR, HD)
    mv[...] = jnp.zeros_like(mv)
    mv[:, 0:HD] = moved.reshape(ROWS, HD)
    cs[...] = mv[pl.ds(FR - 1, FR, stride=FR), :]
    carry_copy = remote(cs, cr, csem.at[0], csem.at[1], s, q_next)
    carry_copy.start()
    for f in range(1, FR):
        lato[pl.ds(f, FR, stride=FR), :] = mv[pl.ds(f - 1, FR, stride=FR), :][:, 0:HD]

    for c in sum((list(t) for p in steps for t in p), x_near + x_far):
        c.wait_send()
    for slot in range(1, 4):
        mix_copy(slot).wait_send()
    for c in (w_wo, w_wu, w_wd):
        c.wait_send()
    for pair in y_pairs + z_sends:
        for c in pair:
            c.wait_send()
    for c in f_copies:
        c.wait_send()

    def gathered(j, carry):
        for c in gathers(j):
            c.wait_send()
        return carry

    lax.fori_loop(0, NC, gathered, 0)
    carry_copy.wait()
    lato[pl.ds(0, FR, stride=FR), :] = jnp.where(q == 0, noise[...], cr[:, 0:HD])


def scratch():
    v = pltpu.VMEM
    dma = pltpu.SemaphoreType.DMA
    return [
        v((HD, D), BF), v((32, D), BF), v((6, 32, D), BF), v((3 * HS, D), BF), v((HD, D), BF),
        v((4 * HS, D), BF), v((D, 4 * FS), BF), v((4 * FS, D), BF),
        v((4, 16, M1), BF), v((4, 16, M2), BF), v((4, 16, M1), BF), v((4, 16, M2), BF),
        v((4, 16, M1), BF), v((4, 16, M2), BF), v((16, M1), BF), v((16, M2), BF),
        v((4, 16, M1), BF), v((4, 16, M2), BF), v((FR, 2 * D), F32), v((FR, 4 * D), F32),
        v((ROWS, 128), F32), v((4, 4, ROWS, 128), BF), v((FR * HD, TOK), BF),
        v((3 * HS, FR * HD), F32), v((3 * HS, 16), F32), v((FR * HD, CW), BF),
        v((3 * HS, FR * HD), BF),
        v((3, HD, TOK), BF), v((3, TOK, HD), BF), v((3, HD + 16, TOK), BF),
        v((4, HS, GROUP), BF), v((4, HS, GROUP), BF), v((4, GROUP, HS), BF),
        v((ROWS, D), F32), v((ROWS, D), F32), v((ROWS, D), BF), v((ROWS, D), BF), v((ROWS, D), BF),
        v((32, D), F32), v((32, D), F32),
        v((ROWS, D), BF), v((ROWS, D), BF), v((32, D), BF), v((32, D), BF),
        v((ROWS, D), BF), v((ROWS, D), BF), v((32, D), BF), v((32, D), BF),
        v((GROUP, D), BF), v((GROUP, 4 * FS), F32), v((GROUP, 4 * FS), BF),
        v((ROWS, 128), F32), v((FR, 128), F32), v((FR, 128), F32),
        dma((8,)), dma((3,)), dma((3,)), dma((9, 2)), dma((9, 2)), dma((9, 2)), dma((9, 2)),
        dma((9,)), dma((9,)), dma((3, 2, 4)), dma((3, 2, 4)), dma((2, 4)), dma((2, 4)),
        dma((4,)), dma((4,)),
        dma((6, NC)), dma((6, NC)), dma((6, NC)), dma((6, NC)), dma((6, NC)), dma((6, NC)),
        dma((2,)),
    ]


def body(
    latents, fresh_noise, levels, patch_weight, time_weight, adaln_weight, qkv_weight,
    out_weight, up_weight, down_weight, proj_weight,
):
    vm = pl.BlockSpec(memory_space=pltpu.VMEM)
    hbm = pl.BlockSpec(memory_space=pl.ANY)
    pred, lato = pl.pallas_call(
        kernel,
        out_shape=(
            jax.ShapeDtypeStruct((ROWS, HD), F32),
            jax.ShapeDtypeStruct((ROWS, HD), F32),
        ),
        in_specs=[pl.BlockSpec(memory_space=pltpu.SMEM), vm, vm] + [hbm] * 8,
        out_specs=(vm, vm),
        scratch_shapes=scratch(),
        compiler_params=pltpu.CompilerParams(
            collective_id=0, has_side_effects=True, vmem_limit_bytes=60 * 1024 * 1024
        ),
    )(
        levels.T,
        latents.reshape(ROWS, HD),
        fresh_noise.reshape(FR, HD),
        patch_weight,
        time_weight.T,
        jnp.transpose(adaln_weight, (1, 0, 2)),
        jnp.transpose(qkv_weight, (1, 2, 0)).reshape(3 * HS, D),
        out_weight,
        up_weight,
        down_weight,
        proj_weight.T,
    )
    return lato.reshape(1, 8, FR, HD), pred.reshape(1, 1, 8, FR, HD)


def solution(mesh):
    in_specs = (
        P("queue", "space", None, None),
        P(None, "space", None),
        P(),
        P(),
        P(None, "space"),
        P("space", None, None),
        P(None, None, "space"),
        P("space", None),
        P(None, "space"),
        P("space", None),
        P(),
    )
    out_specs = (P("queue", "space", None, None), P(None, "queue", "space", None, None))
    return jax.shard_map(body, mesh=mesh, in_specs=in_specs, out_specs=out_specs, check_vma=False)
```

```python
import functools
import math

import jax
import jax.numpy as jnp
from jax import lax
from jax.experimental import pallas as pl
from jax.experimental.pallas import tpu as pltpu
from jax.sharding import PartitionSpec as P

MESH = pl.DeviceIdType.MESH
BF = jnp.bfloat16
F32 = jnp.float32
HD = 64
NT = 1000
NQ = 16
NS = 16
D = 3072
FR = 8
ROWS = 64
TOK = 1024
GROUP = 256
NC = 4
CW = D // NC
NK = 2
CK = D // NK
HR = ROWS // 2
QR = HR // 2
GR = GROUP // 2
FS = 384
HS = 192
M1 = 2 * D // 8
M2 = 4 * D // 8


def noise_level(times):
    angle = (times / NT + 0.008) / 1.008 * (math.pi / 2)
    cosine = jnp.cos(angle)
    return 0.05 + 0.94 * cosine * cosine


def dot_nt(a, b):
    return lax.dot_general(a, b, (((1,), (1,)), ((), ())), preferred_element_type=F32)


def dot(a, b):
    return jnp.dot(a, b, preferred_element_type=F32)


def lnorm(v):
    centre = v - jnp.mean(v, -1, keepdims=True)
    spread = jnp.mean(centre * centre, -1, keepdims=True)
    return centre * lax.rsqrt(spread + 1e-05)


def kernel(
    lev, lat, noise, patch_h, tw_h, ada_h, qkv_h, out_h, up_h, down_h, proj_h,
    both,
    patch, tw, ada, qkv, proj, wo, wu, wd,
    p1, p2, ra1, ra2, rb1, rb2, b1, b2, t1, t2, mod1, mod2,
    xs, xg, xet, acc_m, acc_s, abuf, mt, qt, kn, va, msend, mixt, mixa,
    res, own, s_o, s_r, s_l, p_r, p_l, rl, rr, ol, or_,
    nbuf, hacc, hid, fin, mv, cs, cr,
    lsem, ps, pr, ys, yr, zs, zr, fs, fr, mss, msr, xss, xrs,
    as_, ar, ss, sr, gs, gr, csem,
):
    q = lax.axis_index("queue")
    s = lax.axis_index("space")
    core = lax.rem(s, 2)
    x = lax.rem(s // 2, 4)
    y = s // 8

    def at(y_, x_, c_):
        return (y_ * 4 + x_) * 2 + c_

    mate = at(y, x, 1 - core)
    over = at(1 - y, x, core)
    q_flip = q + 1 - 2 * lax.rem(q, 2)
    right = at(y, lax.rem(x + 1, 4), core)
    left = at(y, lax.rem(x + 3, 4), core)
    q_next = lax.rem(q + 1, NQ)
    q_prev = lax.rem(q + NQ - 1, NQ)

    def local(i, src, dst):
        return pltpu.make_async_copy(src, dst, lsem.at[i])

    def remote(src, dst, ssem, rsem, sp, qq=None):
        return pltpu.make_async_remote_copy(
            src_ref=src, dst_ref=dst, send_sem=ssem, recv_sem=rsem,
            device_id=(q if qq is None else qq, sp), device_id_type=MESH,
        )

    c_tw = local(0, tw_h, tw)
    c_ada = local(1, ada_h, ada)
    c_patch = local(2, patch_h, patch)
    c_qkv = local(3, qkv_h, qkv)
    c_wo = local(4, out_h, wo.at[pl.ds(0, HS)])
    c_wu = local(5, up_h, wu.at[:, pl.ds(0, FS)])
    c_wd = local(6, down_h, wd.at[pl.ds(0, FS)])
    c_proj = local(7, proj_h, proj)
    for c in (c_tw, c_ada, c_patch, c_qkv):
        c.start()

    bar = pltpu.get_barrier_semaphore()

    group = ((mate, 1), (over, 2), (at(1 - y, x, 1 - core), 3))
    ring = ((right, 1), (at(y, lax.rem(x + 2, 4), core), 2), (left, 3))
    par = lax.rem(q // 2, 2)
    z_to = [lax.rem(q + NQ + 2 * (1 - 2 * par) * (1 - 2 * h), NQ) for h in range(2)]
    for dev in (
        [(q, o) for o, _ in group + ring]
        + [(q_flip, over), (q_next, s), (q_prev, s), (z_to[0], s), (z_to[1], s)]
    ):
        pl.semaphore_signal(bar, inc=1, device_id=dev, device_id_type=MESH)

    row = lax.broadcasted_iota(jnp.int32, (FR, 128), 0)
    now = jnp.zeros((FR, 128), F32)
    later = jnp.zeros((FR, 128), F32)
    for f in range(FR):
        t_now = lev[f, q].astype(F32)
        if f < FR - 1:
            t_later = lev[f + 1, q].astype(F32)
        else:
            t_later = lev[0, jnp.minimum(q + 1, NQ - 1)].astype(F32)
        now = jnp.where(row == f, t_now, now)
        later = jnp.where(row == f, t_later, later)
    a_now = noise_level(now)
    a_after = noise_level(later)
    a_after = jnp.where((row == FR - 1) & (q == NQ - 1), 1.0, a_after)
    keep = jnp.sqrt(a_after / a_now)
    mix = jnp.sqrt(1.0 - a_after) - jnp.sqrt(a_after * (1.0 - a_now) / a_now)

    half = D // 2
    lane = lax.broadcasted_iota(jnp.int32, (FR, half), 1).astype(F32)
    freqs = jnp.exp(-math.log(10000.0) * lane / half)
    angle = now[:, 0:1] * freqs
    c_tw.wait()
    pre = dot_nt(jnp.cos(angle).astype(BF), tw[:, 0:half]) + dot_nt(
        jnp.sin(angle).astype(BF), tw[:, half:D]
    )
    timing = (pre * jax.nn.sigmoid(pre)).astype(BF)
    c_ada.wait()
    for k in range(2):
        part = dot(timing, ada[k])
        for h in range(2):
            two = [part[:, (2 * h + i) * M1 : (2 * h + i + 1) * M1] for i in range(2)]
            p1[2 * k + h] = jnp.concatenate(two, 0).astype(BF)

    me4 = y * 2 + core
    pl.semaphore_wait(bar, 11)

    def slot_of(slot):
        return lax.rem(y + slot // 2, 2) * 2 + lax.rem(core + slot, 2)

    def group_sum(k, part, recv):
        ssem, rsem = mss.at[0, k], msr.at[0, k]
        return [
            remote(part.at[slot_of(i)], recv.at[i], ssem.at[i], rsem.at[i], o) for o, i in group
        ]

    def ring_sum(k, mine, recv):
        ssem, rsem = mss.at[1, k], msr.at[1, k]
        return [remote(mine, recv.at[i], ssem.at[i], rsem.at[i], o) for o, i in ring]

    def group_spread(k, tot):
        ssem, rsem = mss.at[2, k], msr.at[2, k]
        return [
            remote(tot.at[me4], tot.at[me4], ssem.at[i], rsem.at[i], o) for o, i in group
        ]

    x_near = [
        remote(xg.at[x, me4], xg.at[x, me4], xss.at[0, i], xrs.at[0, i], o) for o, i in group
    ]
    x_far = [remote(xg.at[x], xg.at[x], xss.at[1, i], xrs.at[1, i], o) for o, i in ring]

    def begin(copies):
        for c in copies:
            c.start()

    def arrive(copies):
        for c in copies:
            c.wait_recv()

    steps = []
    for k, (part, ra, mine, rb, tot) in enumerate(((p1, ra1, b1, rb1, t1), (p2, ra2, b2, rb2, t2))):
        steps.append((group_sum(k, part, ra), ring_sum(k, mine, rb), group_spread(k, tot)))

    def join(k):
        part, ra, mine = ((p1, ra1, b1), (p2, ra2, b2))[k]
        arrive(steps[k][0])
        acc = part[me4].astype(F32)
        for i in range(1, 4):
            acc += ra[i].astype(F32)
        mine[...] = acc.astype(BF)
        begin(steps[k][1])

    def close(k):
        mine, rb, tot = ((b1, rb1, t1), (b2, rb2, t2))[k]
        arrive(steps[k][1])
        acc = mine[...].astype(F32)
        for i in range(1, 4):
            acc += rb[i].astype(F32)
        tot[me4] = acc.astype(BF)
        begin(steps[k][2])

    def unpack(k):
        tot, mod, w = ((t1, mod1, M1), (t2, mod2, M2))[k]
        arrive(steps[k][2])
        for m in range(4):
            v = tot[m].astype(F32)
            mod[:, 2 * m * w : (2 * m + 1) * w] = v[0:FR]
            mod[:, (2 * m + 1) * w : (2 * m + 2) * w] = v[FR : 2 * FR]

    begin(steps[0][0])

    c_patch.wait()
    x_own = lat[...]
    res[...] = dot(x_own.astype(BF), patch[...])
    full = res[...]
    centre = full - jnp.mean(full, -1, keepdims=True)
    spread = jnp.mean(centre * centre, -1, keepdims=True)
    rstd = lax.rsqrt(spread + 1e-05)
    r_hi = rstd.astype(BF).astype(F32)
    r_mid = (rstd - r_hi).astype(BF).astype(F32)
    r_lo = rstd - r_hi - r_mid
    xs[...] = jnp.zeros_like(xs)
    xs[:, 0:HD] = x_own
    lane_x = lax.broadcasted_iota(jnp.int32, (ROWS, 128), 1)
    packed = xs[...]
    packed = jnp.where(lane_x == 64, r_hi, packed)
    packed = jnp.where(lane_x == 65, r_mid, packed)
    packed = jnp.where(lane_x == 66, r_lo, packed)
    xg[x, me4] = packed.astype(BF)
    begin(x_near)

    w_wo = remote(out_h, wo.at[pl.ds(HS, HS)], ps.at[0], pr.at[0], mate)
    w_wu = remote(up_h, wu.at[:, pl.ds(FS, FS)], ps.at[1], pr.at[1], mate)
    w_wd = remote(down_h, wd.at[pl.ds(FS, FS)], ps.at[2], pr.at[2], mate)

    y_pairs = []
    z_sends = []
    z_recvs = []
    f_copies = []

    def piece(i, source, target, forward_from, forward_to):
        mine = [2 * par + h for h in range(2)]
        theirs = [2 * (1 - par) + h for h in range(2)]
        y_pairs.append([
            remote(source(mine[h]), target(mine[h]), ys.at[i, h], yr.at[i, h], over, (q, q_flip)[h])
            for h in range(2)
        ])
        for lst, parts in ((z_sends, mine), (z_recvs, theirs)):
            lst.append([
                remote(target(parts[h]), target(parts[h]), zs.at[i, h], zr.at[i, h], s, z_to[h])
                for h in range(2)
            ])
        f_copies.append(remote(forward_from, forward_to, fs.at[i], fr.at[i], mate))

    def rows_of(base, part, size):
        return pl.ds(pl.multiple_of(base + part * size, 16), size)

    piece(
        0,
        lambda p: out_h.at[rows_of(0, p, HS // 4)],
        lambda p: wo.at[rows_of(2 * HS, p, HS // 4)],
        wo.at[pl.ds(2 * HS, HS)],
        wo.at[pl.ds(3 * HS, HS)],
    )
    for k in range(NC):
        piece(
            1 + k,
            lambda p, k=k: up_h.at[rows_of(k * CW, p, CW // 4)],
            lambda p, k=k: wu.at[rows_of(k * CW, p, CW // 4), pl.ds(2 * FS, FS)],
            wu.at[pl.ds(k * CW, CW), pl.ds(2 * FS, FS)],
            wu.at[pl.ds(k * CW, CW), pl.ds(3 * FS, FS)],
        )
    for k in range(NC):
        piece(
            1 + NC + k,
            lambda p, k=k: down_h.at[rows_of(0, p, FS // 4), pl.ds(k * CW, CW)],
            lambda p, k=k: wd.at[rows_of(2 * FS, p, FS // 4), pl.ds(k * CW, CW)],
            wd.at[pl.ds(2 * FS, FS), pl.ds(k * CW, CW)],
            wd.at[pl.ds(3 * FS, FS), pl.ds(k * CW, CW)],
        )

    def push(i):
        begin(y_pairs[i])

    def along(i):
        arrive(y_pairs[i])
        begin(z_sends[i])

    def forward(i):
        arrive(z_recvs[i])
        f_copies[i].start()

    c_wo.start()
    push(0)
    w_wo.start()
    c_proj.start()

    for k in range(4):
        part = dot(timing, ada[2 + k])
        p2[k] = jnp.concatenate([part[:, 0:M2], part[:, M2 : 2 * M2]], 0).astype(BF)
    join(0)
    arrive(x_near)
    begin(x_far)
    close(0)
    begin(steps[1][0])
    for k in range(NC):
        push(1 + k)
    c_wu.start()
    w_wu.start()

    arrive(x_far)
    halves = [
        xg[b, m, h * HR : (h + 1) * HR] for h in range(2) for m in range(4) for b in range(4)
    ]
    xt = jnp.concatenate(halves, 0).astype(F32).T
    rstd_all = xt[64:65] + xt[65:66] + xt[66:67]
    frame = lax.rem(lax.broadcasted_iota(jnp.int32, (HD, TOK), 1), FR)
    xt = xt[0:HD]
    for f in range(FR):
        xet[f * HD : (f + 1) * HD, :] = jnp.where(frame == f, xt, 0.0).astype(BF)
    hot = (
        lax.rem(lax.broadcasted_iota(jnp.int32, (16, TOK), 1), FR)
        == lax.rem(lax.broadcasted_iota(jnp.int32, (16, TOK), 0), FR)
    ).astype(F32).astype(BF)

    acc_m[...] = jnp.zeros_like(acc_m)
    acc_s[...] = jnp.zeros_like(acc_s)
    hacc[...] = jnp.zeros_like(hacc)
    mean_w = jnp.mean(patch[...].astype(F32), -1, keepdims=True)
    c_qkv.wait()
    unpack(0)
    along(0)

    def fold(j, carry):
        c = pl.ds(pl.multiple_of(j * CW, 128), CW)
        centred = patch[:, c].astype(F32) - mean_w
        gain = 1.0 + mod1[:, pl.ds(pl.multiple_of(D + j * CW, 128), CW)]
        for f in range(FR):
            abuf[f * HD : (f + 1) * HD, :] = (centred * gain[f : f + 1]).astype(BF)
        shift = mod1[:, c]
        hi = shift.astype(BF).astype(F32)
        both = jnp.concatenate([hi, shift - hi], 0).astype(BF)
        w = qkv[:, c]
        acc_m[...] += dot_nt(w, abuf[...])
        acc_s[...] += dot_nt(w, both)
        return carry

    join(1)
    lax.fori_loop(0, NC, fold, 0)
    along(1)
    along(2)
    close(1)
    mt[...] = acc_m[...].astype(BF)
    s_hi = acc_s[...].astype(BF)
    s_lo = (acc_s[...] - s_hi.astype(F32)).astype(BF)

    def project(k):
        r = slice(k * HS, (k + 1) * HS)
        out = dot(mt[r, :], xet[...]) * rstd_all
        return (out + dot(s_hi[r], hot) + dot(s_lo[r], hot)).reshape(3, HD, TOK)

    def head_norm(v):
        centre = v - jnp.mean(v, 1, keepdims=True)
        spread = jnp.mean(centre * centre, 1, keepdims=True)
        return centre * lax.rsqrt(spread + 1e-06)

    queries = head_norm(project(0)) * (HD**-0.5 / math.log(2.0))
    qt[...] = queries.astype(BF)
    keys = head_norm(project(1))
    for h in range(3):
        kn[h] = keys[h].T.astype(BF)
    values = project(2)
    for h in range(3):
        va[h, 0:HD, :] = values[h].astype(BF)
        va[h, HD : HD + 16, :] = jnp.ones((16, TOK), BF)

    def mix_copies(h):
        return [
            remote(msend.at[h, 0, 1 - core], mixt.at[h, 1], as_.at[h, 1], ar.at[h, 1], mate),
            remote(msend.at[h, 1, core], mixt.at[h, 2], as_.at[h, 2], ar.at[h, 2], over),
            remote(msend.at[h, 1, 1 - core], mixt.at[h, 3], as_.at[h, 3], ar.at[h, 3], group[2][0]),
        ]

    def attend(h):
        def part(i, carry):
            flip = 1 - i
            y_ = lax.rem(y + flip, 2)
            g = pl.ds(pl.multiple_of((h * 2 + y_) * GROUP, GROUP), GROUP)
            for n in range(3):
                scores = dot(kn[n], qt[n, :, g])
                weights = jnp.exp2(scores).astype(BF)
                o = dot(va[n], weights)
                o = (o[0:HD] / o[HD : HD + 1]).astype(BF)
                for c in range(2):
                    msend[h, flip, c, n * HD : (n + 1) * HD, :] = o[:, c * GR : (c + 1) * GR]

            @pl.when(i == 0)
            def _():
                begin(mix_copies(h)[1:])

            return carry

        lax.fori_loop(0, 2, part, 0)
        begin(mix_copies(h)[:1])

    def turn(h):
        mixt[h, 0] = msend[h, 0, core]
        arrive(mix_copies(h))
        v = mixt[h].reshape(4 * HS, GR).astype(F32).T.astype(BF)
        for b in range(4):
            o = lax.rem(b - x + 4, 4)
            r = pl.ds(pl.multiple_of(o * HR, HR), HR)
            mixa[h, r, :] = v[b * HR : (b + 1) * HR]

    def chunk(j):
        return pl.ds(pl.multiple_of(j * CK, 128), CK)

    lo, hi16 = pl.ds(0, QR), pl.ds(QR, QR)

    def sends(p, h, j):
        c = chunk(j)

        def to(i, src, rows, dst, dst_rows, dev):
            return remote(
                src.at[h, rows, c], dst.at[p, h, dst_rows, c], ss.at[p, h, j, i], sr.at[p, h, j, i], dev
            )

        return [
            to(0, s_o, lo, ol, lo, right),
            to(1, s_o, hi16, or_, lo, left),
            to(2, s_r, hi16, rl, hi16, right),
            to(3, s_l, lo, rr, lo, left),
            to(4, s_r, lo, rl, lo, right),
            to(5, s_l, hi16, rr, hi16, left),
        ]

    def opened(p, h, term):
        def step(j, carry):
            c = chunk(j)
            v = term(h, c)
            m = sends(p, h, j)
            s_o[h, :, c] = v[2 * HR : 3 * HR].astype(BF)
            begin(m[0:2])
            s_r[h, QR:HR, c] = v[HR + QR : 2 * HR].astype(BF)
            s_l[h, 0:QR, c] = v[3 * HR : 3 * HR + QR].astype(BF)
            begin(m[2:4])
            p_r[h, :, c] = v[HR : HR + QR]
            p_l[h, :, c] = v[3 * HR + QR : 4 * HR]
            own[h, :, c] = v[0:HR]
            return carry

        lax.fori_loop(0, NK, step, 0)

    def passed(p, h):
        def step(j, carry):
            c = chunk(j)
            m = sends(p, h, j)
            m[0].wait_recv()
            s_r[h, 0:QR, c] = (p_r[h, :, c] + ol[p, h, :, c].astype(F32)).astype(BF)
            m[4].start()
            m[1].wait_recv()
            s_l[h, QR:HR, c] = (p_l[h, :, c] + or_[p, h, :, c].astype(F32)).astype(BF)
            m[5].start()
            return carry

        lax.fori_loop(0, NK, step, 0)

    def finish(p, h):
        def step(j, carry):
            arrive(sends(p, h, j)[2:])
            return carry

        lax.fori_loop(0, NK, step, 0)

    def sent(p, h):
        def step(j, carry):
            for c in sends(p, h, j):
                c.wait_send()
            return carry

        lax.fori_loop(0, NK, step, 0)

    def update(i, p, h, gate):
        r = pl.ds(pl.multiple_of(i * 16, 16), 16)
        rows = pl.ds(pl.multiple_of(h * HR + i * 16, 16), 16)
        summed = own[h, r, :] + rl[p, h, r, :].astype(F32) + rr[p, h, r, :].astype(F32)
        gated = mod2[:, gate * D : (gate + 1) * D] * summed.reshape(2, FR, D)
        return r, rows, res[rows, :].reshape(2, FR, D) + gated

    def second(h):
        def step(i, carry):
            r, rows, new = update(i, 0, h, 0)
            res[rows, :] = new.reshape(16, D)
            v = lnorm(new) * (1.0 + mod2[:, 2 * D : 3 * D]) + mod2[:, D : 2 * D]
            nbuf[h, r, :] = v.reshape(16, D).astype(BF)
            return carry

        lax.fori_loop(0, HR // 16, step, 0)

    def last(h):
        def step(i, carry):
            _, rows, new = update(i, 1, h, 3)
            fin[rows, :] = lnorm(new).reshape(16, D).astype(BF)
            return carry

        lax.fori_loop(0, HR // 16, step, 0)

    def gathers(h, j):
        c = chunk(j)

        def go(i, src, dst, dev):
            return remote(
                nbuf.at[h, pl.ds(src, QR), c], nbuf.at[h, pl.ds(dst, QR), c],
                gs.at[h, j, i], gr.at[h, j, i], dev,
            )

        return [
            go(0, 0, 3 * HR, right),
            go(1, QR, HR + QR, left),
            go(2, QR, 3 * HR + QR, right),
            go(3, 0, HR, left),
            go(4, 3 * HR, 2 * HR, right),
            go(5, HR + QR, 2 * HR + QR, left),
        ]

    def gather(h):
        def step(j, carry):
            begin(gathers(h, j)[:4])
            return carry

        lax.fori_loop(0, NK, step, 0)

    def relay(h, j):
        m = gathers(h, j)
        m[0].wait_recv()
        m[4].start()
        m[1].wait_recv()
        m[5].start()

    def widen(h, j):
        arrive(gathers(h, j)[2:])

        def step(n, carry):
            c = pl.ds(pl.multiple_of(n * 512, 512), 512)
            hacc[h, :, c] += dot(nbuf[h, :, j * CK : (j + 1) * CK], wu[j * CK : (j + 1) * CK, c])
            return carry

        lax.fori_loop(0, 3, step, 0)

    def activate(h):
        def step(i, carry):
            r = pl.ds(pl.multiple_of(i * 16, 16), 16)
            hid[h, r, :] = jax.nn.gelu(hacc[h, r, :], approximate=True).astype(BF)
            return carry

        lax.fori_loop(0, GR // 16, step, 0)

    def out_term(h, c):
        return dot(mixa[h], wo[:, c])

    def down_term(h, c):
        return dot(hid[h], wd[:, c])

    attend(0)
    along(3)
    along(4)
    attend(1)
    for k in range(NC):
        push(1 + NC + k)
    forward(0)
    turn(0)
    c_wo.wait()
    w_wo.wait_recv()
    f_copies[0].wait_recv()
    opened(0, 0, out_term)
    turn(1)
    c_wd.start()
    w_wd.start()
    passed(0, 0)
    opened(0, 1, out_term)
    unpack(1)
    forward(1)
    forward(2)
    passed(0, 1)
    along(1 + NC)
    along(2 + NC)
    finish(0, 0)
    second(0)
    gather(0)
    forward(3)
    forward(4)
    finish(0, 1)
    second(1)
    gather(1)
    along(3 + NC)
    along(4 + NC)
    for j in range(NK):
        relay(0, j)
    sent(0, 0)
    sent(0, 1)
    c_wu.wait()
    w_wu.wait_recv()
    for k in range(NC):
        f_copies[1 + k].wait_recv()
    widen(0, 0)
    relay(1, 0)
    widen(0, 1)
    relay(1, 1)
    activate(0)
    for k in range(NC):
        forward(1 + NC + k)
    c_wd.wait()
    w_wd.wait_recv()
    for k in range(NC):
        f_copies[1 + NC + k].wait_recv()
    opened(1, 0, down_term)
    widen(1, 0)
    widen(1, 1)
    activate(1)
    passed(1, 0)
    opened(1, 1, down_term)
    passed(1, 1)
    finish(1, 0)
    last(0)
    finish(1, 1)
    last(1)
    c_proj.wait()
    out = dot_nt(fin[...], proj[...])
    both[0] = out
    moved = keep[:, 0:HD] * lat[...].reshape(FR, FR, HD) + mix[:, 0:HD] * out.reshape(FR, FR, HD)
    mv[...] = jnp.zeros_like(mv)
    mv[:, 0:HD] = moved.reshape(ROWS, HD)
    cs[...] = mv[pl.ds(FR - 1, FR, stride=FR), :]
    carry_copy = remote(cs, cr, csem.at[0], csem.at[1], s, q_next)
    carry_copy.start()
    for f in range(1, FR):
        both[1, pl.ds(f, FR, stride=FR), :] = mv[pl.ds(f - 1, FR, stride=FR), :][:, 0:HD]

    for c in sum((list(t) for p in steps for t in p), x_near + x_far):
        c.wait_send()
    for h in range(2):
        for c in mix_copies(h):
            c.wait_send()
        sent(1, h)
    for c in (w_wo, w_wu, w_wd):
        c.wait_send()
    for pair in y_pairs + z_sends:
        for c in pair:
            c.wait_send()
    for c in f_copies:
        c.wait_send()

    for h in range(2):
        for j in range(NK):
            for c in gathers(h, j):
                c.wait_send()
    carry_copy.wait()
    both[1, pl.ds(0, FR, stride=FR), :] = jnp.where(q == 0, noise[...], cr[:, 0:HD])


def scratch():
    v = pltpu.VMEM
    dma = pltpu.SemaphoreType.DMA
    return [
        v((HD, D), BF), v((32, D), BF), v((6, 32, D), BF), v((3 * HS, D), BF), v((HD, D), BF),
        v((4 * HS, D), BF), v((D, 4 * FS), BF), v((4 * FS, D), BF),
        v((4, 16, M1), BF), v((4, 16, M2), BF), v((4, 16, M1), BF), v((4, 16, M2), BF),
        v((4, 16, M1), BF), v((4, 16, M2), BF), v((16, M1), BF), v((16, M2), BF),
        v((4, 16, M1), BF), v((4, 16, M2), BF), v((FR, 2 * D), F32), v((FR, 4 * D), F32),
        v((ROWS, 128), F32), v((4, 4, ROWS, 128), BF), v((FR * HD, TOK), BF),
        v((3 * HS, FR * HD), F32), v((3 * HS, 16), F32), v((FR * HD, CW), BF),
        v((3 * HS, FR * HD), BF),
        v((3, HD, TOK), BF), v((3, TOK, HD), BF), v((3, HD + 16, TOK), BF),
        v((2, 2, 2, HS, GR), BF), v((2, 4, HS, GR), BF), v((2, GR, 4 * HS), BF),
        v((ROWS, D), F32), v((2, HR, D), F32),
        v((2, HR, D), BF), v((2, HR, D), BF), v((2, HR, D), BF),
        v((2, QR, D), F32), v((2, QR, D), F32),
        v((2, 2, HR, D), BF), v((2, 2, HR, D), BF), v((2, 2, QR, D), BF), v((2, 2, QR, D), BF),
        v((2, GR, D), BF), v((2, GR, 4 * FS), F32), v((2, GR, 4 * FS), BF), v((ROWS, D), BF),
        v((ROWS, 128), F32), v((FR, 128), F32), v((FR, 128), F32),
        dma((8,)), dma((3,)), dma((3,)), dma((9, 2)), dma((9, 2)), dma((9, 2)), dma((9, 2)),
        dma((9,)), dma((9,)), dma((3, 2, 4)), dma((3, 2, 4)), dma((2, 4)), dma((2, 4)),
        dma((2, 4)), dma((2, 4)),
        dma((2, 2, NK, 6)), dma((2, 2, NK, 6)), dma((2, NK, 6)), dma((2, NK, 6)),
        dma((2,)),
    ]


def body(
    latents, fresh_noise, levels, patch_weight, time_weight, adaln_weight, qkv_weight,
    out_weight, up_weight, down_weight, proj_weight,
):
    vm = pl.BlockSpec(memory_space=pltpu.VMEM)
    hbm = pl.BlockSpec(memory_space=pl.ANY)
    both = pl.pallas_call(
        kernel,
        out_shape=jax.ShapeDtypeStruct((2, ROWS, HD), F32),
        in_specs=[pl.BlockSpec(memory_space=pltpu.SMEM), vm, vm] + [hbm] * 8,
        out_specs=vm,
        scratch_shapes=scratch(),
        compiler_params=pltpu.CompilerParams(
            collective_id=0, has_side_effects=True, vmem_limit_bytes=60 * 1024 * 1024
        ),
    )(
        levels.T,
        latents.reshape(ROWS, HD),
        fresh_noise.reshape(FR, HD),
        patch_weight,
        time_weight.T,
        jnp.transpose(adaln_weight, (1, 0, 2)),
        jnp.transpose(qkv_weight, (1, 2, 0)).reshape(3 * HS, D),
        out_weight,
        up_weight,
        down_weight,
        proj_weight.T,
    )
    return both[1].reshape(1, 8, FR, HD), both[0].reshape(1, 1, 8, FR, HD)


def solution(mesh):
    in_specs = (
        P("queue", "space", None, None),
        P(None, "space", None),
        P(),
        P(),
        P(None, "space"),
        P("space", None, None),
        P(None, None, "space"),
        P("space", None),
        P(None, "space"),
        P("space", None),
        P(),
    )
    out_specs = (P("queue", "space", None, None), P(None, "queue", "space", None, None))
    return jax.shard_map(body, mesh=mesh, in_specs=in_specs, out_specs=out_specs, check_vma=False)
```

```python
import functools
import math

import jax
import jax.numpy as jnp
from jax import lax
from jax.experimental import pallas as pl
from jax.experimental.pallas import tpu as pltpu
from jax.sharding import PartitionSpec as P

MESH = pl.DeviceIdType.MESH
BF = jnp.bfloat16
F32 = jnp.float32
HD = 64
NT = 1000
NQ = 16
NS = 16
D = 3072
FR = 8
ROWS = 64
TOK = 1024
GROUP = 256
NC = 4
CW = D // NC
NK = 2
CK = D // NK
HR = ROWS // 2
QR = HR // 2
GR = GROUP // 2
FS = 384
HS = 192
M1 = 2 * D // 8
M2 = 4 * D // 8


def noise_level(times):
    angle = (times / NT + 0.008) / 1.008 * (math.pi / 2)
    cosine = jnp.cos(angle)
    return 0.05 + 0.94 * cosine * cosine


def dot_nt(a, b):
    return lax.dot_general(a, b, (((1,), (1,)), ((), ())), preferred_element_type=F32)


def dot(a, b):
    return jnp.dot(a, b, preferred_element_type=F32)


def lnorm(v):
    centre = v - jnp.mean(v, -1, keepdims=True)
    spread = jnp.mean(centre * centre, -1, keepdims=True)
    return centre * lax.rsqrt(spread + 1e-05)


def kernel(
    lev, lat, noise, patch_h, tw_h, ada_h, qkv_h, out_h, up_h, down_h, proj_h,
    both,
    patch, tw, ada, qkv, proj, wo, wu, wd,
    p1, p2, ra1, ra2, rb1, rb2, b1, b2, t1, t2, mod1, mod2,
    xs, xg, xet, acc_m, acc_s, abuf, mt, qt, kn, va, msend, mixt, mixa,
    res, own, s_o, s_r, s_l, p_r, p_l, rl, rr, ol, or_,
    nbuf, hacc, hid, fin, mv, cs, cr,
    lsem, ps, pr, ys, yr, zs, zr, fs, fr, mss, msr, xss, xrs,
    as_, ar, ss, sr, gs, gr, csem,
):
    q = lax.axis_index("queue")
    s = lax.axis_index("space")
    core = lax.rem(s, 2)
    x = lax.rem(s // 2, 4)
    y = s // 8

    def at(y_, x_, c_):
        return (y_ * 4 + x_) * 2 + c_

    mate = at(y, x, 1 - core)
    over = at(1 - y, x, core)
    q_flip = q + 1 - 2 * lax.rem(q, 2)
    right = at(y, lax.rem(x + 1, 4), core)
    left = at(y, lax.rem(x + 3, 4), core)
    q_next = lax.rem(q + 1, NQ)
    q_prev = lax.rem(q + NQ - 1, NQ)

    def local(i, src, dst):
        return pltpu.make_async_copy(src, dst, lsem.at[i])

    def remote(src, dst, ssem, rsem, sp, qq=None):
        return pltpu.make_async_remote_copy(
            src_ref=src, dst_ref=dst, send_sem=ssem, recv_sem=rsem,
            device_id=(q if qq is None else qq, sp), device_id_type=MESH,
        )

    c_tw = local(0, tw_h, tw)
    c_ada = local(1, ada_h, ada)
    c_patch = local(2, patch_h, patch)
    c_qkv = local(3, qkv_h, qkv)
    c_wo = local(4, out_h, wo.at[pl.ds(0, HS)])
    c_wu = local(5, up_h, wu.at[:, pl.ds(0, FS)])
    c_wd = local(6, down_h, wd.at[pl.ds(0, FS)])
    c_proj = local(7, proj_h, proj)
    for c in (c_tw, c_ada, c_patch, c_qkv):
        c.start()

    bar = pltpu.get_barrier_semaphore()

    group = ((mate, 1), (over, 2), (at(1 - y, x, 1 - core), 3))
    ring = ((right, 1), (at(y, lax.rem(x + 2, 4), core), 2), (left, 3))
    par = lax.rem(q // 2, 2)
    z_to = [lax.rem(q + NQ + 2 * (1 - 2 * par) * (1 - 2 * h), NQ) for h in range(2)]
    for dev in (
        [(q, o) for o, _ in group + ring]
        + [(q_flip, over), (q_next, s), (q_prev, s), (z_to[0], s), (z_to[1], s)]
    ):
        pl.semaphore_signal(bar, inc=1, device_id=dev, device_id_type=MESH)

    row = lax.broadcasted_iota(jnp.int32, (FR, 128), 0)
    now = jnp.zeros((FR, 128), F32)
    later = jnp.zeros((FR, 128), F32)
    for f in range(FR):
        t_now = lev[f, q].astype(F32)
        if f < FR - 1:
            t_later = lev[f + 1, q].astype(F32)
        else:
            t_later = lev[0, jnp.minimum(q + 1, NQ - 1)].astype(F32)
        now = jnp.where(row == f, t_now, now)
        later = jnp.where(row == f, t_later, later)
    a_now = noise_level(now)
    a_after = noise_level(later)
    a_after = jnp.where((row == FR - 1) & (q == NQ - 1), 1.0, a_after)
    keep = jnp.sqrt(a_after / a_now)
    mix = jnp.sqrt(1.0 - a_after) - jnp.sqrt(a_after * (1.0 - a_now) / a_now)

    half = D // 2
    lane = lax.broadcasted_iota(jnp.int32, (FR, half), 1).astype(F32)
    freqs = jnp.exp(-math.log(10000.0) * lane / half)
    angle = now[:, 0:1] * freqs
    c_tw.wait()
    pre = dot_nt(jnp.cos(angle).astype(BF), tw[:, 0:half]) + dot_nt(
        jnp.sin(angle).astype(BF), tw[:, half:D]
    )
    timing = (pre * jax.nn.sigmoid(pre)).astype(BF)
    c_ada.wait()
    for k in range(2):
        part = dot(timing, ada[k])
        for h in range(2):
            two = [part[:, (2 * h + i) * M1 : (2 * h + i + 1) * M1] for i in range(2)]
            p1[2 * k + h] = jnp.concatenate(two, 0).astype(BF)

    me4 = y * 2 + core
    pl.semaphore_wait(bar, 11)

    def slot_of(slot):
        return lax.rem(y + slot // 2, 2) * 2 + lax.rem(core + slot, 2)

    def group_sum(k, part, recv):
        ssem, rsem = mss.at[0, k], msr.at[0, k]
        return [
            remote(part.at[slot_of(i)], recv.at[i], ssem.at[i], rsem.at[i], o) for o, i in group
        ]

    def ring_sum(k, mine, recv):
        ssem, rsem = mss.at[1, k], msr.at[1, k]
        return [remote(mine, recv.at[i], ssem.at[i], rsem.at[i], o) for o, i in ring]

    def group_spread(k, tot):
        ssem, rsem = mss.at[2, k], msr.at[2, k]
        return [
            remote(tot.at[me4], tot.at[me4], ssem.at[i], rsem.at[i], o) for o, i in group
        ]

    x_near = [
        remote(xg.at[x, me4], xg.at[x, me4], xss.at[0, i], xrs.at[0, i], o) for o, i in group
    ]
    x_far = [remote(xg.at[x], xg.at[x], xss.at[1, i], xrs.at[1, i], o) for o, i in ring]

    def begin(copies):
        for c in copies:
            c.start()

    def arrive(copies):
        for c in copies:
            c.wait_recv()

    steps = []
    for k, (part, ra, mine, rb, tot) in enumerate(((p1, ra1, b1, rb1, t1), (p2, ra2, b2, rb2, t2))):
        steps.append((group_sum(k, part, ra), ring_sum(k, mine, rb), group_spread(k, tot)))

    def join(k):
        part, ra, mine = ((p1, ra1, b1), (p2, ra2, b2))[k]
        arrive(steps[k][0])
        acc = part[me4].astype(F32)
        for i in range(1, 4):
            acc += ra[i].astype(F32)
        mine[...] = acc.astype(BF)
        begin(steps[k][1])

    def close(k):
        mine, rb, tot = ((b1, rb1, t1), (b2, rb2, t2))[k]
        arrive(steps[k][1])
        acc = mine[...].astype(F32)
        for i in range(1, 4):
            acc += rb[i].astype(F32)
        tot[me4] = acc.astype(BF)
        begin(steps[k][2])

    def unpack(k):
        tot, mod, w = ((t1, mod1, M1), (t2, mod2, M2))[k]
        arrive(steps[k][2])
        for m in range(4):
            v = tot[m].astype(F32)
            mod[:, 2 * m * w : (2 * m + 1) * w] = v[0:FR]
            mod[:, (2 * m + 1) * w : (2 * m + 2) * w] = v[FR : 2 * FR]

    begin(steps[0][0])

    c_patch.wait()
    x_own = lat[...]
    res[...] = dot(x_own.astype(BF), patch[...])
    full = res[...]
    centre = full - jnp.mean(full, -1, keepdims=True)
    spread = jnp.mean(centre * centre, -1, keepdims=True)
    rstd = lax.rsqrt(spread + 1e-05)
    r_hi = rstd.astype(BF).astype(F32)
    r_mid = (rstd - r_hi).astype(BF).astype(F32)
    r_lo = rstd - r_hi - r_mid
    xs[...] = jnp.zeros_like(xs)
    xs[:, 0:HD] = x_own
    lane_x = lax.broadcasted_iota(jnp.int32, (ROWS, 128), 1)
    packed = xs[...]
    packed = jnp.where(lane_x == 64, r_hi, packed)
    packed = jnp.where(lane_x == 65, r_mid, packed)
    packed = jnp.where(lane_x == 66, r_lo, packed)
    xg[x, me4] = packed.astype(BF)
    begin(x_near)

    w_wo = remote(out_h, wo.at[pl.ds(HS, HS)], ps.at[0], pr.at[0], mate)
    w_wu = remote(up_h, wu.at[:, pl.ds(FS, FS)], ps.at[1], pr.at[1], mate)
    w_wd = remote(down_h, wd.at[pl.ds(FS, FS)], ps.at[2], pr.at[2], mate)

    y_pairs = []
    z_sends = []
    z_recvs = []
    f_copies = []

    def piece(i, source, target, forward_from, forward_to):
        mine = [2 * par + h for h in range(2)]
        theirs = [2 * (1 - par) + h for h in range(2)]
        y_pairs.append([
            remote(source(mine[h]), target(mine[h]), ys.at[i, h], yr.at[i, h], over, (q, q_flip)[h])
            for h in range(2)
        ])
        for lst, parts in ((z_sends, mine), (z_recvs, theirs)):
            lst.append([
                remote(target(parts[h]), target(parts[h]), zs.at[i, h], zr.at[i, h], s, z_to[h])
                for h in range(2)
            ])
        f_copies.append(remote(forward_from, forward_to, fs.at[i], fr.at[i], mate))

    def rows_of(base, part, size):
        return pl.ds(pl.multiple_of(base + part * size, 16), size)

    piece(
        0,
        lambda p: out_h.at[rows_of(0, p, HS // 4)],
        lambda p: wo.at[rows_of(2 * HS, p, HS // 4)],
        wo.at[pl.ds(2 * HS, HS)],
        wo.at[pl.ds(3 * HS, HS)],
    )
    for k in range(NC):
        piece(
            1 + k,
            lambda p, k=k: up_h.at[rows_of(k * CW, p, CW // 4)],
            lambda p, k=k: wu.at[rows_of(k * CW, p, CW // 4), pl.ds(2 * FS, FS)],
            wu.at[pl.ds(k * CW, CW), pl.ds(2 * FS, FS)],
            wu.at[pl.ds(k * CW, CW), pl.ds(3 * FS, FS)],
        )
    for k in range(NC):
        piece(
            1 + NC + k,
            lambda p, k=k: down_h.at[rows_of(0, p, FS // 4), pl.ds(k * CW, CW)],
            lambda p, k=k: wd.at[rows_of(2 * FS, p, FS // 4), pl.ds(k * CW, CW)],
            wd.at[pl.ds(2 * FS, FS), pl.ds(k * CW, CW)],
            wd.at[pl.ds(3 * FS, FS), pl.ds(k * CW, CW)],
        )

    def push(i):
        begin(y_pairs[i])

    def along(i):
        arrive(y_pairs[i])
        begin(z_sends[i])

    def forward(i):
        arrive(z_recvs[i])
        f_copies[i].start()

    c_wo.start()
    push(0)
    w_wo.start()
    c_proj.start()

    join(0)
    arrive(x_near)
    begin(x_far)
    for k in range(4):
        part = dot(timing, ada[2 + k])
        p2[k] = jnp.concatenate([part[:, 0:M2], part[:, M2 : 2 * M2]], 0).astype(BF)
    close(0)
    begin(steps[1][0])
    c_wu.start()
    w_wu.start()

    arrive(x_far)
    halves = [
        xg[b, m, h * HR : (h + 1) * HR] for h in range(2) for m in range(4) for b in range(4)
    ]
    xt = jnp.concatenate(halves, 0).astype(F32).T
    rstd_all = xt[64:65] + xt[65:66] + xt[66:67]
    frame = lax.rem(lax.broadcasted_iota(jnp.int32, (HD, TOK), 1), FR)
    xt = xt[0:HD]
    for f in range(FR):
        xet[f * HD : (f + 1) * HD, :] = jnp.where(frame == f, xt, 0.0).astype(BF)
    hot = (
        lax.rem(lax.broadcasted_iota(jnp.int32, (16, TOK), 1), FR)
        == lax.rem(lax.broadcasted_iota(jnp.int32, (16, TOK), 0), FR)
    ).astype(F32).astype(BF)

    along(0)
    acc_m[...] = jnp.zeros_like(acc_m)
    acc_s[...] = jnp.zeros_like(acc_s)
    hacc[...] = jnp.zeros_like(hacc)
    mean_w = jnp.mean(patch[...].astype(F32), -1, keepdims=True)
    c_qkv.wait()
    unpack(0)
    push(1)
    push(2)

    def fold(j, carry):
        c = pl.ds(pl.multiple_of(j * CW, 128), CW)
        centred = patch[:, c].astype(F32) - mean_w
        gain = 1.0 + mod1[:, pl.ds(pl.multiple_of(D + j * CW, 128), CW)]
        for f in range(FR):
            abuf[f * HD : (f + 1) * HD, :] = (centred * gain[f : f + 1]).astype(BF)
        shift = mod1[:, c]
        hi = shift.astype(BF).astype(F32)
        both = jnp.concatenate([hi, shift - hi], 0).astype(BF)
        w = qkv[:, c]
        acc_m[...] += dot_nt(w, abuf[...])
        acc_s[...] += dot_nt(w, both)
        return carry

    join(1)
    lax.fori_loop(0, NC, fold, 0)
    close(1)
    mt[...] = acc_m[...].astype(BF)
    s_hi = acc_s[...].astype(BF)
    s_lo = (acc_s[...] - s_hi.astype(F32)).astype(BF)

    def project(k):
        r = slice(k * HS, (k + 1) * HS)
        out = dot(mt[r, :], xet[...]) * rstd_all
        return (out + dot(s_hi[r], hot) + dot(s_lo[r], hot)).reshape(3, HD, TOK)

    def head_norm(v):
        centre = v - jnp.mean(v, 1, keepdims=True)
        spread = jnp.mean(centre * centre, 1, keepdims=True)
        return centre * lax.rsqrt(spread + 1e-06)

    queries = head_norm(project(0)) * (HD**-0.5 / math.log(2.0))
    qt[...] = queries.astype(BF)
    keys = head_norm(project(1))
    for h in range(3):
        kn[h] = keys[h].T.astype(BF)
    values = project(2)
    for h in range(3):
        va[h, 0:HD, :] = values[h].astype(BF)
        va[h, HD : HD + 16, :] = jnp.ones((16, TOK), BF)

    def mix_copies(h):
        return [
            remote(msend.at[h, 0, 1 - core], mixt.at[h, 1], as_.at[h, 1], ar.at[h, 1], mate),
            remote(msend.at[h, 1, core], mixt.at[h, 2], as_.at[h, 2], ar.at[h, 2], over),
            remote(msend.at[h, 1, 1 - core], mixt.at[h, 3], as_.at[h, 3], ar.at[h, 3], group[2][0]),
        ]

    def attend(h):
        def part(i, carry):
            flip = 1 - i
            y_ = lax.rem(y + flip, 2)
            g = pl.ds(pl.multiple_of((h * 2 + y_) * GROUP, GROUP), GROUP)
            for n in range(3):
                asked = qt[n, :, g]
                o = jnp.zeros((HD + 16, GROUP), F32)
                for k in range(4):
                    some = slice(k * GROUP, (k + 1) * GROUP)
                    weights = jnp.exp2(dot(kn[n, some, :], asked)).astype(BF)
                    o += dot(va[n, :, some], weights)
                o = (o[0:HD] / o[HD : HD + 1]).astype(BF)
                for c in range(2):
                    msend[h, flip, c, n * HD : (n + 1) * HD, :] = o[:, c * GR : (c + 1) * GR]

            @pl.when(i == 0)
            def _():
                begin(mix_copies(h)[1:])

            return carry

        lax.fori_loop(0, 2, part, 0)
        begin(mix_copies(h)[:1])

    def turn(h):
        mixt[h, 0] = msend[h, 0, core]
        arrive(mix_copies(h))
        v = mixt[h].reshape(4 * HS, GR).astype(F32).T.astype(BF)
        for b in range(4):
            o = lax.rem(b - x + 4, 4)
            r = pl.ds(pl.multiple_of(o * HR, HR), HR)
            mixa[h, r, :] = v[b * HR : (b + 1) * HR]

    def chunk(j):
        return pl.ds(pl.multiple_of(j * CK, 128), CK)

    lo, hi16 = pl.ds(0, QR), pl.ds(QR, QR)

    def sends(p, h, j):
        c = chunk(j)

        def to(i, src, rows, dst, dst_rows, dev):
            return remote(
                src.at[h, rows, c], dst.at[p, h, dst_rows, c], ss.at[p, h, j, i], sr.at[p, h, j, i], dev
            )

        return [
            to(0, s_o, lo, ol, lo, right),
            to(1, s_o, hi16, or_, lo, left),
            to(2, s_r, hi16, rl, hi16, right),
            to(3, s_l, lo, rr, lo, left),
            to(4, s_r, lo, rl, lo, right),
            to(5, s_l, hi16, rr, hi16, left),
        ]

    def opened(p, h, term, late=()):
        def step(j, carry):
            @pl.when(j > 0)
            def _():
                arrive(late)

            c = chunk(j)
            v = term(h, c)
            m = sends(p, h, j)
            s_o[h, :, c] = v[2 * HR : 3 * HR].astype(BF)
            begin(m[0:2])
            s_r[h, QR:HR, c] = v[HR + QR : 2 * HR].astype(BF)
            s_l[h, 0:QR, c] = v[3 * HR : 3 * HR + QR].astype(BF)
            begin(m[2:4])
            p_r[h, :, c] = v[HR : HR + QR]
            p_l[h, :, c] = v[3 * HR + QR : 4 * HR]
            own[h, :, c] = v[0:HR]
            return carry

        lax.fori_loop(0, NK, step, 0)

    def passed(p, h):
        def step(j, carry):
            c = chunk(j)
            m = sends(p, h, j)
            m[0].wait_recv()
            s_r[h, 0:QR, c] = (p_r[h, :, c] + ol[p, h, :, c].astype(F32)).astype(BF)
            m[4].start()
            m[1].wait_recv()
            s_l[h, QR:HR, c] = (p_l[h, :, c] + or_[p, h, :, c].astype(F32)).astype(BF)
            m[5].start()
            return carry

        lax.fori_loop(0, NK, step, 0)

    def finish(p, h):
        def step(j, carry):
            arrive(sends(p, h, j)[2:])
            return carry

        lax.fori_loop(0, NK, step, 0)

    def sent(p, h):
        def step(j, carry):
            for c in sends(p, h, j):
                c.wait_send()
            return carry

        lax.fori_loop(0, NK, step, 0)

    def update(i, p, h, gate):
        r = pl.ds(pl.multiple_of(i * 16, 16), 16)
        rows = pl.ds(pl.multiple_of(h * HR + i * 16, 16), 16)
        summed = own[h, r, :] + rl[p, h, r, :].astype(F32) + rr[p, h, r, :].astype(F32)
        gated = mod2[:, gate * D : (gate + 1) * D] * summed.reshape(2, FR, D)
        return r, rows, res[rows, :].reshape(2, FR, D) + gated

    def second(h):
        def step(i, carry):
            r, rows, new = update(i, 0, h, 0)
            res[rows, :] = new.reshape(16, D)
            v = lnorm(new) * (1.0 + mod2[:, 2 * D : 3 * D]) + mod2[:, D : 2 * D]
            nbuf[h, r, :] = v.reshape(16, D).astype(BF)
            return carry

        lax.fori_loop(0, HR // 16, step, 0)

    def last(h):
        def step(i, carry):
            _, rows, new = update(i, 1, h, 3)
            fin[rows, :] = lnorm(new).reshape(16, D).astype(BF)
            return carry

        lax.fori_loop(0, HR // 16, step, 0)

    def gathers(h, j):
        c = chunk(j)

        def go(i, src, dst, dev):
            return remote(
                nbuf.at[h, pl.ds(src, QR), c], nbuf.at[h, pl.ds(dst, QR), c],
                gs.at[h, j, i], gr.at[h, j, i], dev,
            )

        return [
            go(0, 0, 3 * HR, right),
            go(1, QR, HR + QR, left),
            go(2, QR, 3 * HR + QR, right),
            go(3, 0, HR, left),
            go(4, 3 * HR, 2 * HR, right),
            go(5, HR + QR, 2 * HR + QR, left),
        ]

    def gather(h):
        def step(j, carry):
            begin(gathers(h, j)[:4])
            return carry

        lax.fori_loop(0, NK, step, 0)

    def relay(h, j):
        m = gathers(h, j)
        m[0].wait_recv()
        m[4].start()
        m[1].wait_recv()
        m[5].start()

    def widen(h, j):
        arrive(gathers(h, j)[2:])

        def step(n, carry):
            c = pl.ds(pl.multiple_of(n * 512, 512), 512)
            hacc[h, :, c] += dot(nbuf[h, :, j * CK : (j + 1) * CK], wu[j * CK : (j + 1) * CK, c])
            return carry

        lax.fori_loop(0, 3, step, 0)

    def activate(h):
        def step(i, carry):
            r = pl.ds(pl.multiple_of(i * 16, 16), 16)
            hid[h, r, :] = jax.nn.gelu(hacc[h, r, :], approximate=True).astype(BF)
            return carry

        lax.fori_loop(0, GR // 16, step, 0)

    def out_term(h, c):
        return dot(mixa[h], wo[:, c])

    def down_term(h, c):
        return dot(hid[h], wd[:, c])

    forward(0)
    attend(0)
    along(1)
    along(2)
    attend(1)
    turn(0)
    push(3)
    push(4)
    c_wo.wait()
    w_wo.wait_recv()
    f_copies[0].wait_recv()
    opened(0, 0, out_term)
    turn(1)
    for k in range(NC):
        push(1 + NC + k)
    c_wd.start()
    w_wd.start()
    passed(0, 0)
    opened(0, 1, out_term)
    unpack(1)
    forward(1)
    forward(2)
    passed(0, 1)
    along(3)
    along(4)
    finish(0, 0)
    second(0)
    gather(0)
    finish(0, 1)
    second(1)
    gather(1)
    forward(3)
    forward(4)
    along(1 + NC)
    along(2 + NC)
    for j in range(NK):
        relay(0, j)
    sent(0, 0)
    sent(0, 1)
    c_wu.wait()
    w_wu.wait_recv()
    for k in range(NC):
        f_copies[1 + k].wait_recv()
    along(3 + NC)
    along(4 + NC)
    widen(0, 0)
    relay(1, 0)
    forward(1 + NC)
    forward(2 + NC)
    widen(0, 1)
    relay(1, 1)
    activate(0)
    forward(3 + NC)
    forward(4 + NC)
    c_wd.wait()
    w_wd.wait_recv()
    arrive(f_copies[1 + NC : 3 + NC])
    opened(1, 0, down_term, f_copies[3 + NC :])
    widen(1, 0)
    widen(1, 1)
    activate(1)
    passed(1, 0)
    opened(1, 1, down_term)
    passed(1, 1)
    finish(1, 0)
    last(0)
    finish(1, 1)
    last(1)
    c_proj.wait()
    out = dot_nt(fin[...], proj[...])
    both[0] = out
    moved = keep[:, 0:HD] * lat[...].reshape(FR, FR, HD) + mix[:, 0:HD] * out.reshape(FR, FR, HD)
    mv[...] = jnp.zeros_like(mv)
    mv[:, 0:HD] = moved.reshape(ROWS, HD)
    cs[...] = mv[pl.ds(FR - 1, FR, stride=FR), :]
    carry_copy = remote(cs, cr, csem.at[0], csem.at[1], s, q_next)
    carry_copy.start()
    for f in range(1, FR):
        both[1, pl.ds(f, FR, stride=FR), :] = mv[pl.ds(f - 1, FR, stride=FR), :][:, 0:HD]

    for c in sum((list(t) for p in steps for t in p), x_near + x_far):
        c.wait_send()
    for h in range(2):
        for c in mix_copies(h):
            c.wait_send()
        sent(1, h)
    for c in (w_wo, w_wu, w_wd):
        c.wait_send()
    for pair in y_pairs + z_sends:
        for c in pair:
            c.wait_send()
    for c in f_copies:
        c.wait_send()

    for h in range(2):
        for j in range(NK):
            for c in gathers(h, j):
                c.wait_send()
    carry_copy.wait()
    both[1, pl.ds(0, FR, stride=FR), :] = jnp.where(q == 0, noise[...], cr[:, 0:HD])


def scratch():
    v = pltpu.VMEM
    dma = pltpu.SemaphoreType.DMA
    return [
        v((HD, D), BF), v((32, D), BF), v((6, 32, D), BF), v((3 * HS, D), BF), v((HD, D), BF),
        v((4 * HS, D), BF), v((D, 4 * FS), BF), v((4 * FS, D), BF),
        v((4, 16, M1), BF), v((4, 16, M2), BF), v((4, 16, M1), BF), v((4, 16, M2), BF),
        v((4, 16, M1), BF), v((4, 16, M2), BF), v((16, M1), BF), v((16, M2), BF),
        v((4, 16, M1), BF), v((4, 16, M2), BF), v((FR, 2 * D), F32), v((FR, 4 * D), F32),
        v((ROWS, 128), F32), v((4, 4, ROWS, 128), BF), v((FR * HD, TOK), BF),
        v((3 * HS, FR * HD), F32), v((3 * HS, 16), F32), v((FR * HD, CW), BF),
        v((3 * HS, FR * HD), BF),
        v((3, HD, TOK), BF), v((3, TOK, HD), BF), v((3, HD + 16, TOK), BF),
        v((2, 2, 2, HS, GR), BF), v((2, 4, HS, GR), BF), v((2, GR, 4 * HS), BF),
        v((ROWS, D), F32), v((2, HR, D), F32),
        v((2, HR, D), BF), v((2, HR, D), BF), v((2, HR, D), BF),
        v((2, QR, D), F32), v((2, QR, D), F32),
        v((2, 2, HR, D), BF), v((2, 2, HR, D), BF), v((2, 2, QR, D), BF), v((2, 2, QR, D), BF),
        v((2, GR, D), BF), v((2, GR, 4 * FS), F32), v((2, GR, 4 * FS), BF), v((ROWS, D), BF),
        v((ROWS, 128), F32), v((FR, 128), F32), v((FR, 128), F32),
        dma((8,)), dma((3,)), dma((3,)), dma((9, 2)), dma((9, 2)), dma((9, 2)), dma((9, 2)),
        dma((9,)), dma((9,)), dma((3, 2, 4)), dma((3, 2, 4)), dma((2, 4)), dma((2, 4)),
        dma((2, 4)), dma((2, 4)),
        dma((2, 2, NK, 6)), dma((2, 2, NK, 6)), dma((2, NK, 6)), dma((2, NK, 6)),
        dma((2,)),
    ]


def body(
    latents, fresh_noise, levels, patch_weight, time_weight, adaln_weight, qkv_weight,
    out_weight, up_weight, down_weight, proj_weight,
):
    vm = pl.BlockSpec(memory_space=pltpu.VMEM)
    hbm = pl.BlockSpec(memory_space=pl.ANY)
    both = pl.pallas_call(
        kernel,
        out_shape=jax.ShapeDtypeStruct((2, ROWS, HD), F32),
        in_specs=[pl.BlockSpec(memory_space=pltpu.SMEM), vm, vm] + [hbm] * 8,
        out_specs=vm,
        scratch_shapes=scratch(),
        compiler_params=pltpu.CompilerParams(
            collective_id=0, has_side_effects=True, vmem_limit_bytes=60 * 1024 * 1024
        ),
    )(
        levels.T,
        latents.reshape(ROWS, HD),
        fresh_noise.reshape(FR, HD),
        patch_weight,
        time_weight.T,
        jnp.transpose(adaln_weight, (1, 0, 2)),
        jnp.transpose(qkv_weight, (1, 2, 0)).reshape(3 * HS, D),
        out_weight,
        up_weight,
        down_weight,
        proj_weight.T,
    )
    return both[1].reshape(1, 8, FR, HD), both[0].reshape(1, 1, 8, FR, HD)


def solution(mesh):
    in_specs = (
        P("queue", "space", None, None),
        P(None, "space", None),
        P(),
        P(),
        P(None, "space"),
        P("space", None, None),
        P(None, None, "space"),
        P("space", None),
        P(None, "space"),
        P("space", None),
        P(),
    )
    out_specs = (P("queue", "space", None, None), P(None, "queue", "space", None, None))
    return jax.shard_map(body, mesh=mesh, in_specs=in_specs, out_specs=out_specs, check_vma=False)
```

```python
import functools
import math

import jax
import jax.numpy as jnp
from jax import lax
from jax.experimental import pallas as pl
from jax.experimental.pallas import tpu as pltpu
from jax.sharding import PartitionSpec as P

MESH = pl.DeviceIdType.MESH
BF = jnp.bfloat16
F32 = jnp.float32
HD = 64
NT = 1000
NQ = 16
NS = 16
D = 3072
FR = 8
ROWS = 64
TOK = 1024
GROUP = 256
NC = 4
CW = D // NC
NK = 2
CK = D // NK
HR = ROWS // 2
QR = HR // 2
GR = GROUP // 2
FS = 384
HS = 192
M1 = 2 * D // 8
M2 = 4 * D // 8


def noise_level(times):
    angle = (times / NT + 0.008) / 1.008 * (math.pi / 2)
    cosine = jnp.cos(angle)
    return 0.05 + 0.94 * cosine * cosine


def dot_nt(a, b):
    return lax.dot_general(a, b, (((1,), (1,)), ((), ())), preferred_element_type=F32)


def dot(a, b):
    return jnp.dot(a, b, preferred_element_type=F32)


def lnorm(v):
    centre = v - jnp.mean(v, -1, keepdims=True)
    spread = jnp.mean(centre * centre, -1, keepdims=True)
    return centre * lax.rsqrt(spread + 1e-05)


def kernel(
    lev, lat, noise, patch_h, tw_h, ada_h, qkv_h, out_h, up_h, down_h, proj_h,
    both,
    patch, tw, ada, qkv, proj, wo, wu, wd,
    p1, p2, ra1, ra2, rb1, rb2, b1, b2, t1, t2, mod1, mod2,
    xs, xg, xet, acc_m, acc_s, abuf, mt, qt, kn, va, msend, mixt, mixa,
    res, own, s_o, s_r, s_l, p_r, p_l, rl, rr, ol, or_,
    nbuf, hacc, hid, fin, mv, cs, cr,
    lsem, ps, pr, ys, yr, zs, zr, fs, fr, mss, msr, xss, xrs,
    as_, ar, ss, sr, gs, gr, csem,
):
    q = lax.axis_index("queue")
    s = lax.axis_index("space")
    core = lax.rem(s, 2)
    x = lax.rem(s // 2, 4)
    y = s // 8

    def at(y_, x_, c_):
        return (y_ * 4 + x_) * 2 + c_

    mate = at(y, x, 1 - core)
    over = at(1 - y, x, core)
    q_flip = q + 1 - 2 * lax.rem(q, 2)
    right = at(y, lax.rem(x + 1, 4), core)
    left = at(y, lax.rem(x + 3, 4), core)
    q_next = lax.rem(q + 1, NQ)
    q_prev = lax.rem(q + NQ - 1, NQ)

    def local(i, src, dst):
        return pltpu.make_async_copy(src, dst, lsem.at[i])

    def remote(src, dst, ssem, rsem, sp, qq=None):
        return pltpu.make_async_remote_copy(
            src_ref=src, dst_ref=dst, send_sem=ssem, recv_sem=rsem,
            device_id=(q if qq is None else qq, sp), device_id_type=MESH,
        )

    c_tw = local(0, tw_h, tw)
    c_ada = local(1, ada_h, ada)
    c_patch = local(2, patch_h, patch)
    c_qkv = local(3, qkv_h, qkv)
    c_wo = local(4, out_h, wo.at[pl.ds(0, HS)])
    c_wu = local(5, up_h, wu.at[:, pl.ds(0, FS)])
    c_wd = local(6, down_h, wd.at[pl.ds(0, FS)])
    c_proj = local(7, proj_h, proj)
    for c in (c_tw, c_ada, c_patch, c_qkv):
        c.start()

    bar = pltpu.get_barrier_semaphore()

    group = ((mate, 1), (over, 2), (at(1 - y, x, 1 - core), 3))
    ring = ((right, 1), (at(y, lax.rem(x + 2, 4), core), 2), (left, 3))
    par = lax.rem(q // 2, 2)
    z_to = [lax.rem(q + NQ + 2 * (1 - 2 * par) * (1 - 2 * h), NQ) for h in range(2)]
    for dev in (
        [(q, o) for o, _ in group + ring]
        + [(q_flip, over), (q_next, s), (q_prev, s), (z_to[0], s), (z_to[1], s)]
    ):
        pl.semaphore_signal(bar, inc=1, device_id=dev, device_id_type=MESH)

    row = lax.broadcasted_iota(jnp.int32, (FR, 128), 0)
    now = jnp.zeros((FR, 128), F32)
    later = jnp.zeros((FR, 128), F32)
    for f in range(FR):
        t_now = lev[f, q].astype(F32)
        if f < FR - 1:
            t_later = lev[f + 1, q].astype(F32)
        else:
            t_later = lev[0, jnp.minimum(q + 1, NQ - 1)].astype(F32)
        now = jnp.where(row == f, t_now, now)
        later = jnp.where(row == f, t_later, later)
    a_now = noise_level(now)
    a_after = noise_level(later)
    a_after = jnp.where((row == FR - 1) & (q == NQ - 1), 1.0, a_after)
    keep = jnp.sqrt(a_after / a_now)
    mix = jnp.sqrt(1.0 - a_after) - jnp.sqrt(a_after * (1.0 - a_now) / a_now)

    half = D // 2
    lane = lax.broadcasted_iota(jnp.int32, (FR, half), 1).astype(F32)
    freqs = jnp.exp(-math.log(10000.0) * lane / half)
    angle = now[:, 0:1] * freqs
    c_tw.wait()
    pre = dot_nt(jnp.cos(angle).astype(BF), tw[:, 0:half]) + dot_nt(
        jnp.sin(angle).astype(BF), tw[:, half:D]
    )
    timing = (pre * jax.nn.sigmoid(pre)).astype(BF)
    c_ada.wait()
    for k in range(2):
        part = dot(timing, ada[k])
        for h in range(2):
            two = [part[:, (2 * h + i) * M1 : (2 * h + i + 1) * M1] for i in range(2)]
            p1[2 * k + h] = jnp.concatenate(two, 0).astype(BF)

    me4 = y * 2 + core
    pl.semaphore_wait(bar, 11)

    def slot_of(slot):
        return lax.rem(y + slot // 2, 2) * 2 + lax.rem(core + slot, 2)

    def group_sum(k, part, recv):
        ssem, rsem = mss.at[0, k], msr.at[0, k]
        return [
            remote(part.at[slot_of(i)], recv.at[i], ssem.at[i], rsem.at[i], o) for o, i in group
        ]

    def ring_sum(k, mine, recv):
        ssem, rsem = mss.at[1, k], msr.at[1, k]
        return [remote(mine, recv.at[i], ssem.at[i], rsem.at[i], o) for o, i in ring]

    def group_spread(k, tot):
        ssem, rsem = mss.at[2, k], msr.at[2, k]
        return [
            remote(tot.at[me4], tot.at[me4], ssem.at[i], rsem.at[i], o) for o, i in group
        ]

    x_near = [
        remote(xg.at[x, me4], xg.at[x, me4], xss.at[0, i], xrs.at[0, i], o) for o, i in group
    ]
    x_far = [remote(xg.at[x], xg.at[x], xss.at[1, i], xrs.at[1, i], o) for o, i in ring]

    def begin(copies):
        for c in copies:
            c.start()

    def arrive(copies):
        for c in copies:
            c.wait_recv()

    steps = []
    for k, (part, ra, mine, rb, tot) in enumerate(((p1, ra1, b1, rb1, t1), (p2, ra2, b2, rb2, t2))):
        steps.append((group_sum(k, part, ra), ring_sum(k, mine, rb), group_spread(k, tot)))

    def join(k):
        part, ra, mine = ((p1, ra1, b1), (p2, ra2, b2))[k]
        arrive(steps[k][0])
        acc = part[me4].astype(F32)
        for i in range(1, 4):
            acc += ra[i].astype(F32)
        mine[...] = acc.astype(BF)
        begin(steps[k][1])

    def close(k):
        mine, rb, tot = ((b1, rb1, t1), (b2, rb2, t2))[k]
        arrive(steps[k][1])
        acc = mine[...].astype(F32)
        for i in range(1, 4):
            acc += rb[i].astype(F32)
        tot[me4] = acc.astype(BF)
        begin(steps[k][2])

    def unpack(k):
        tot, mod, w = ((t1, mod1, M1), (t2, mod2, M2))[k]
        arrive(steps[k][2])
        for m in range(4):
            v = tot[m].astype(F32)
            mod[:, 2 * m * w : (2 * m + 1) * w] = v[0:FR]
            mod[:, (2 * m + 1) * w : (2 * m + 2) * w] = v[FR : 2 * FR]

    begin(steps[0][0])

    c_patch.wait()
    x_own = lat[...]
    res[...] = dot(x_own.astype(BF), patch[...])
    full = res[...]
    centre = full - jnp.mean(full, -1, keepdims=True)
    spread = jnp.mean(centre * centre, -1, keepdims=True)
    rstd = lax.rsqrt(spread + 1e-05)
    r_hi = rstd.astype(BF).astype(F32)
    r_mid = (rstd - r_hi).astype(BF).astype(F32)
    r_lo = rstd - r_hi - r_mid
    xs[...] = jnp.zeros_like(xs)
    xs[:, 0:HD] = x_own
    lane_x = lax.broadcasted_iota(jnp.int32, (ROWS, 128), 1)
    packed = xs[...]
    packed = jnp.where(lane_x == 64, r_hi, packed)
    packed = jnp.where(lane_x == 65, r_mid, packed)
    packed = jnp.where(lane_x == 66, r_lo, packed)
    xg[x, me4] = packed.astype(BF)
    begin(x_near)

    w_wo = remote(out_h, wo.at[pl.ds(HS, HS)], ps.at[0], pr.at[0], mate)
    w_wu = remote(up_h, wu.at[:, pl.ds(FS, FS)], ps.at[1], pr.at[1], mate)
    w_wd = remote(down_h, wd.at[pl.ds(FS, FS)], ps.at[2], pr.at[2], mate)

    y_pairs = []
    z_sends = []
    z_recvs = []
    f_copies = []

    def piece(i, source, target, forward_from, forward_to):
        mine = [2 * par + h for h in range(2)]
        theirs = [2 * (1 - par) + h for h in range(2)]
        y_pairs.append([
            remote(source(mine[h]), target(mine[h]), ys.at[i, h], yr.at[i, h], over, (q, q_flip)[h])
            for h in range(2)
        ])
        for lst, parts in ((z_sends, mine), (z_recvs, theirs)):
            lst.append([
                remote(target(parts[h]), target(parts[h]), zs.at[i, h], zr.at[i, h], s, z_to[h])
                for h in range(2)
            ])
        f_copies.append(remote(forward_from, forward_to, fs.at[i], fr.at[i], mate))

    def rows_of(base, part, size):
        return pl.ds(pl.multiple_of(base + part * size, 16), size)

    piece(
        0,
        lambda p: out_h.at[rows_of(0, p, HS // 4)],
        lambda p: wo.at[rows_of(2 * HS, p, HS // 4)],
        wo.at[pl.ds(2 * HS, HS)],
        wo.at[pl.ds(3 * HS, HS)],
    )
    for k in range(NC):
        piece(
            1 + k,
            lambda p, k=k: up_h.at[rows_of(k * CW, p, CW // 4)],
            lambda p, k=k: wu.at[rows_of(k * CW, p, CW // 4), pl.ds(2 * FS, FS)],
            wu.at[pl.ds(k * CW, CW), pl.ds(2 * FS, FS)],
            wu.at[pl.ds(k * CW, CW), pl.ds(3 * FS, FS)],
        )
    for k in range(NC):
        piece(
            1 + NC + k,
            lambda p, k=k: down_h.at[rows_of(0, p, FS // 4), pl.ds(k * CW, CW)],
            lambda p, k=k: wd.at[rows_of(2 * FS, p, FS // 4), pl.ds(k * CW, CW)],
            wd.at[pl.ds(2 * FS, FS), pl.ds(k * CW, CW)],
            wd.at[pl.ds(3 * FS, FS), pl.ds(k * CW, CW)],
        )

    def push(i):
        begin(y_pairs[i])

    def along(i):
        arrive(y_pairs[i])
        begin(z_sends[i])

    def forward(i):
        arrive(z_recvs[i])
        f_copies[i].start()

    c_wo.start()
    push(0)
    w_wo.start()
    c_proj.start()

    join(0)
    arrive(x_near)
    begin(x_far)
    for k in range(4):
        part = dot(timing, ada[2 + k])
        p2[k] = jnp.concatenate([part[:, 0:M2], part[:, M2 : 2 * M2]], 0).astype(BF)
    close(0)
    begin(steps[1][0])
    c_wu.start()
    w_wu.start()

    arrive(x_far)
    halves = [
        xg[b, m, h * HR : (h + 1) * HR] for h in range(2) for m in range(4) for b in range(4)
    ]
    xt = jnp.concatenate(halves, 0).astype(F32).T
    rstd_all = xt[64:65] + xt[65:66] + xt[66:67]
    frame = lax.rem(lax.broadcasted_iota(jnp.int32, (HD, TOK), 1), FR)
    xt = xt[0:HD]
    for f in range(FR):
        xet[f * HD : (f + 1) * HD, :] = jnp.where(frame == f, xt, 0.0).astype(BF)
    hot = (
        lax.rem(lax.broadcasted_iota(jnp.int32, (32, TOK), 1), FR)
        == lax.rem(lax.broadcasted_iota(jnp.int32, (32, TOK), 0), FR)
    ).astype(F32).astype(BF)

    along(0)
    acc_m[...] = jnp.zeros_like(acc_m)
    acc_s[...] = jnp.zeros_like(acc_s)
    hacc[...] = jnp.zeros_like(hacc)
    mean_w = jnp.mean(patch[...].astype(F32), -1, keepdims=True)
    c_qkv.wait()
    unpack(0)
    push(1)
    push(2)

    def fold_one(j, b):
        c = pl.ds(pl.multiple_of(j * CW, 128), CW)
        centred = patch[:, c].astype(F32) - mean_w
        gain = 1.0 + mod1[:, pl.ds(pl.multiple_of(D + j * CW, 128), CW)]
        for f in range(FR):
            abuf[b, f * HD : (f + 1) * HD, :] = (centred * gain[f : f + 1]).astype(BF)
        shift = mod1[:, c]
        hi = shift.astype(BF).astype(F32)
        both = jnp.concatenate([hi, shift - hi], 0).astype(BF)
        w = qkv[:, c]
        acc_m[...] += dot_nt(w, abuf[b])
        acc_s[...] += dot_nt(w, both)

    def fold(i, carry):
        fold_one(2 * i, 0)
        fold_one(2 * i + 1, 1)
        return carry

    join(1)
    lax.fori_loop(0, NC // 2, fold, 0)
    close(1)
    mt[...] = acc_m[...].astype(BF)
    s_hi = acc_s[...].astype(BF)
    s_lo = (acc_s[...] - s_hi.astype(F32)).astype(BF)
    s_all = jnp.concatenate([s_hi, s_lo], 1)

    def project(k):
        r = slice(k * HS, (k + 1) * HS)
        out = dot(mt[r, :], xet[...]) * rstd_all
        return (out + dot(s_all[r], hot)).reshape(3, HD, TOK)

    def head_norm(v):
        centre = v - jnp.mean(v, 1, keepdims=True)
        spread = jnp.mean(centre * centre, 1, keepdims=True)
        return centre * lax.rsqrt(spread + 1e-06)

    queries = head_norm(project(0)) * (HD**-0.5 / math.log(2.0))
    qt[...] = queries.astype(BF)
    keys = head_norm(project(1))
    for h in range(3):
        kn[h] = keys[h].T.astype(BF)
    values = project(2)
    for h in range(3):
        va[h, 0:HD, :] = values[h].astype(BF)
        va[h, HD : HD + 16, :] = jnp.ones((16, TOK), BF)

    def mix_copies(h):
        return [
            remote(msend.at[h, 0, 1 - core], mixt.at[h, 1], as_.at[h, 1], ar.at[h, 1], mate),
            remote(msend.at[h, 1, core], mixt.at[h, 2], as_.at[h, 2], ar.at[h, 2], over),
            remote(msend.at[h, 1, 1 - core], mixt.at[h, 3], as_.at[h, 3], ar.at[h, 3], group[2][0]),
        ]

    def attend(h):
        def part(i, carry):
            flip = 1 - i
            y_ = lax.rem(y + flip, 2)
            g = pl.ds(pl.multiple_of((h * 2 + y_) * GROUP, GROUP), GROUP)
            for n in range(3):
                asked = qt[n, :, g]
                o = jnp.zeros((HD + 16, GROUP), F32)
                for k in range(4):
                    some = slice(k * GROUP, (k + 1) * GROUP)
                    weights = jnp.exp2(dot(kn[n, some, :], asked)).astype(BF)
                    o += dot(va[n, :, some], weights)
                o = (o[0:HD] / o[HD : HD + 1]).astype(BF)
                for c in range(2):
                    msend[h, flip, c, n * HD : (n + 1) * HD, :] = o[:, c * GR : (c + 1) * GR]

            @pl.when(i == 0)
            def _():
                begin(mix_copies(h)[1:])

            return carry

        lax.fori_loop(0, 2, part, 0)
        begin(mix_copies(h)[:1])

    def turn(h):
        mixt[h, 0] = msend[h, 0, core]
        arrive(mix_copies(h))
        v = mixt[h].reshape(4 * HS, GR).astype(F32).T.astype(BF)
        for b in range(4):
            o = lax.rem(b - x + 4, 4)
            r = pl.ds(pl.multiple_of(o * HR, HR), HR)
            mixa[h, r, :] = v[b * HR : (b + 1) * HR]

    def chunk(j):
        return pl.ds(pl.multiple_of(j * CK, 128), CK)

    lo, hi16 = pl.ds(0, QR), pl.ds(QR, QR)

    def sends(p, h, j):
        c = chunk(j)

        def to(i, src, rows, dst, dst_rows, dev):
            return remote(
                src.at[h, rows, c], dst.at[p, h, dst_rows, c], ss.at[p, h, j, i], sr.at[p, h, j, i], dev
            )

        return [
            to(0, s_o, lo, ol, lo, right),
            to(1, s_o, hi16, or_, lo, left),
            to(2, s_r, hi16, rl, hi16, right),
            to(3, s_l, lo, rr, lo, left),
            to(4, s_r, lo, rl, lo, right),
            to(5, s_l, hi16, rr, hi16, left),
        ]

    def opened(p, h, term, late=()):
        def step(j, carry):
            @pl.when(j > 0)
            def _():
                arrive(late)

            c = chunk(j)
            v = term(h, c)
            m = sends(p, h, j)
            s_o[h, :, c] = v[2 * HR : 3 * HR].astype(BF)
            begin(m[0:2])
            s_r[h, QR:HR, c] = v[HR + QR : 2 * HR].astype(BF)
            s_l[h, 0:QR, c] = v[3 * HR : 3 * HR + QR].astype(BF)
            begin(m[2:4])
            p_r[h, :, c] = v[HR : HR + QR]
            p_l[h, :, c] = v[3 * HR + QR : 4 * HR]
            own[h, :, c] = v[0:HR]
            return carry

        lax.fori_loop(0, NK, step, 0)

    def passed(p, h):
        def step(j, carry):
            c = chunk(j)
            m = sends(p, h, j)
            m[0].wait_recv()
            s_r[h, 0:QR, c] = (p_r[h, :, c] + ol[p, h, :, c].astype(F32)).astype(BF)
            m[4].start()
            m[1].wait_recv()
            s_l[h, QR:HR, c] = (p_l[h, :, c] + or_[p, h, :, c].astype(F32)).astype(BF)
            m[5].start()
            return carry

        lax.fori_loop(0, NK, step, 0)

    def finish(p, h):
        def step(j, carry):
            arrive(sends(p, h, j)[2:])
            return carry

        lax.fori_loop(0, NK, step, 0)

    def sent(p, h):
        def step(j, carry):
            for c in sends(p, h, j):
                c.wait_send()
            return carry

        lax.fori_loop(0, NK, step, 0)

    def update(i, p, h, gate):
        r = pl.ds(pl.multiple_of(i * 16, 16), 16)
        rows = pl.ds(pl.multiple_of(h * HR + i * 16, 16), 16)
        summed = own[h, r, :] + rl[p, h, r, :].astype(F32) + rr[p, h, r, :].astype(F32)
        gated = mod2[:, gate * D : (gate + 1) * D] * summed.reshape(2, FR, D)
        return r, rows, res[rows, :].reshape(2, FR, D) + gated

    def second(h):
        def step(i, carry):
            r, rows, new = update(i, 0, h, 0)
            res[rows, :] = new.reshape(16, D)
            v = lnorm(new) * (1.0 + mod2[:, 2 * D : 3 * D]) + mod2[:, D : 2 * D]
            nbuf[h, r, :] = v.reshape(16, D).astype(BF)
            return carry

        lax.fori_loop(0, HR // 16, step, 0)

    def last(h):
        def step(i, carry):
            _, rows, new = update(i, 1, h, 3)
            fin[rows, :] = lnorm(new).reshape(16, D).astype(BF)
            return carry

        lax.fori_loop(0, HR // 16, step, 0)

    def gathers(h, j):
        c = chunk(j)

        def go(i, src, dst, dev):
            return remote(
                nbuf.at[h, pl.ds(src, QR), c], nbuf.at[h, pl.ds(dst, QR), c],
                gs.at[h, j, i], gr.at[h, j, i], dev,
            )

        return [
            go(0, 0, 3 * HR, right),
            go(1, QR, HR + QR, left),
            go(2, QR, 3 * HR + QR, right),
            go(3, 0, HR, left),
            go(4, 3 * HR, 2 * HR, right),
            go(5, HR + QR, 2 * HR + QR, left),
        ]

    def gather(h):
        def step(j, carry):
            begin(gathers(h, j)[:4])
            return carry

        lax.fori_loop(0, NK, step, 0)

    def relay(h, j):
        m = gathers(h, j)
        m[0].wait_recv()
        m[4].start()
        m[1].wait_recv()
        m[5].start()

    def widen(h, j):
        arrive(gathers(h, j)[2:])

        def step(n, carry):
            c = pl.ds(pl.multiple_of(n * 512, 512), 512)
            hacc[h, :, c] += dot(nbuf[h, :, j * CK : (j + 1) * CK], wu[j * CK : (j + 1) * CK, c])
            return carry

        lax.fori_loop(0, 3, step, 0)

    def activate(h):
        def step(i, carry):
            r = pl.ds(pl.multiple_of(i * 16, 16), 16)
            hid[h, r, :] = jax.nn.gelu(hacc[h, r, :], approximate=True).astype(BF)
            return carry

        lax.fori_loop(0, GR // 16, step, 0)

    def out_term(h, c):
        return dot(mixa[h], wo[:, c])

    def down_term(h, c):
        return dot(hid[h], wd[:, c])

    forward(0)
    attend(0)
    along(1)
    along(2)
    attend(1)
    push(3)
    push(4)
    turn(0)
    c_wo.wait()
    w_wo.wait_recv()
    f_copies[0].wait_recv()
    opened(0, 0, out_term)
    turn(1)
    for k in range(NC):
        push(1 + NC + k)
    c_wd.start()
    w_wd.start()
    passed(0, 0)
    opened(0, 1, out_term)
    unpack(1)
    forward(1)
    forward(2)
    along(3)
    along(4)
    passed(0, 1)
    finish(0, 0)
    second(0)
    gather(0)
    finish(0, 1)
    second(1)
    gather(1)
    forward(3)
    forward(4)
    along(1 + NC)
    along(2 + NC)
    for j in range(NK):
        relay(0, j)
    sent(0, 0)
    sent(0, 1)
    c_wu.wait()
    w_wu.wait_recv()
    arrive(f_copies[1:3])
    along(3 + NC)
    along(4 + NC)
    widen(0, 0)
    relay(1, 0)
    forward(1 + NC)
    forward(2 + NC)
    arrive(f_copies[3:5])
    widen(0, 1)
    relay(1, 1)
    activate(0)
    forward(3 + NC)
    forward(4 + NC)
    c_wd.wait()
    w_wd.wait_recv()
    arrive(f_copies[1 + NC : 3 + NC])
    opened(1, 0, down_term, f_copies[3 + NC :])
    widen(1, 0)
    widen(1, 1)
    activate(1)
    passed(1, 0)
    opened(1, 1, down_term)
    passed(1, 1)
    finish(1, 0)
    last(0)
    finish(1, 1)
    last(1)
    c_proj.wait()
    out = dot_nt(fin[...], proj[...])
    both[0] = out
    moved = keep[:, 0:HD] * lat[...].reshape(FR, FR, HD) + mix[:, 0:HD] * out.reshape(FR, FR, HD)
    mv[...] = jnp.zeros_like(mv)
    mv[:, 0:HD] = moved.reshape(ROWS, HD)
    cs[...] = mv[pl.ds(FR - 1, FR, stride=FR), :]
    carry_copy = remote(cs, cr, csem.at[0], csem.at[1], s, q_next)
    carry_copy.start()
    for f in range(1, FR):
        both[1, pl.ds(f, FR, stride=FR), :] = mv[pl.ds(f - 1, FR, stride=FR), :][:, 0:HD]

    for c in sum((list(t) for p in steps for t in p), x_near + x_far):
        c.wait_send()
    for h in range(2):
        for c in mix_copies(h):
            c.wait_send()
        sent(1, h)
    for c in (w_wo, w_wu, w_wd):
        c.wait_send()
    for pair in y_pairs + z_sends:
        for c in pair:
            c.wait_send()
    for c in f_copies:
        c.wait_send()

    for h in range(2):
        for j in range(NK):
            for c in gathers(h, j):
                c.wait_send()
    carry_copy.wait()
    both[1, pl.ds(0, FR, stride=FR), :] = jnp.where(q == 0, noise[...], cr[:, 0:HD])


def scratch():
    v = pltpu.VMEM
    dma = pltpu.SemaphoreType.DMA
    return [
        v((HD, D), BF), v((32, D), BF), v((6, 32, D), BF), v((3 * HS, D), BF), v((HD, D), BF),
        v((4 * HS, D), BF), v((D, 4 * FS), BF), v((4 * FS, D), BF),
        v((4, 16, M1), BF), v((4, 16, M2), BF), v((4, 16, M1), BF), v((4, 16, M2), BF),
        v((4, 16, M1), BF), v((4, 16, M2), BF), v((16, M1), BF), v((16, M2), BF),
        v((4, 16, M1), BF), v((4, 16, M2), BF), v((FR, 2 * D), F32), v((FR, 4 * D), F32),
        v((ROWS, 128), F32), v((4, 4, ROWS, 128), BF), v((FR * HD, TOK), BF),
        v((3 * HS, FR * HD), F32), v((3 * HS, 16), F32), v((2, FR * HD, CW), BF),
        v((3 * HS, FR * HD), BF),
        v((3, HD, TOK), BF), v((3, TOK, HD), BF), v((3, HD + 16, TOK), BF),
        v((2, 2, 2, HS, GR), BF), v((2, 4, HS, GR), BF), v((2, GR, 4 * HS), BF),
        v((ROWS, D), F32), v((2, HR, D), F32),
        v((2, HR, D), BF), v((2, HR, D), BF), v((2, HR, D), BF),
        v((2, QR, D), F32), v((2, QR, D), F32),
        v((2, 2, HR, D), BF), v((2, 2, HR, D), BF), v((2, 2, QR, D), BF), v((2, 2, QR, D), BF),
        v((2, GR, D), BF), v((2, GR, 4 * FS), F32), v((2, GR, 4 * FS), BF), v((ROWS, D), BF),
        v((ROWS, 128), F32), v((FR, 128), F32), v((FR, 128), F32),
        dma((8,)), dma((3,)), dma((3,)), dma((9, 2)), dma((9, 2)), dma((9, 2)), dma((9, 2)),
        dma((9,)), dma((9,)), dma((3, 2, 4)), dma((3, 2, 4)), dma((2, 4)), dma((2, 4)),
        dma((2, 4)), dma((2, 4)),
        dma((2, 2, NK, 6)), dma((2, 2, NK, 6)), dma((2, NK, 6)), dma((2, NK, 6)),
        dma((2,)),
    ]


def body(
    latents, fresh_noise, levels, patch_weight, time_weight, adaln_weight, qkv_weight,
    out_weight, up_weight, down_weight, proj_weight,
):
    vm = pl.BlockSpec(memory_space=pltpu.VMEM)
    hbm = pl.BlockSpec(memory_space=pl.ANY)
    both = pl.pallas_call(
        kernel,
        out_shape=jax.ShapeDtypeStruct((2, ROWS, HD), F32),
        in_specs=[pl.BlockSpec(memory_space=pltpu.SMEM), vm, vm] + [hbm] * 8,
        out_specs=vm,
        scratch_shapes=scratch(),
        compiler_params=pltpu.CompilerParams(
            collective_id=0, has_side_effects=True, vmem_limit_bytes=60 * 1024 * 1024
        ),
    )(
        levels.T,
        latents.reshape(ROWS, HD),
        fresh_noise.reshape(FR, HD),
        patch_weight,
        time_weight.T,
        jnp.transpose(adaln_weight, (1, 0, 2)),
        jnp.transpose(qkv_weight, (1, 2, 0)).reshape(3 * HS, D),
        out_weight,
        up_weight,
        down_weight,
        proj_weight.T,
    )
    return both[1].reshape(1, 8, FR, HD), both[0].reshape(1, 1, 8, FR, HD)


def solution(mesh):
    in_specs = (
        P("queue", "space", None, None),
        P(None, "space", None),
        P(),
        P(),
        P(None, "space"),
        P("space", None, None),
        P(None, None, "space"),
        P("space", None),
        P(None, "space"),
        P("space", None),
        P(),
    )
    out_specs = (P("queue", "space", None, None), P(None, "queue", "space", None, None))
    return jax.shard_map(body, mesh=mesh, in_specs=in_specs, out_specs=out_specs, check_vma=False)
```

```python
import functools
import math

import jax
import jax.numpy as jnp
from jax import lax
from jax.experimental import pallas as pl
from jax.experimental.pallas import tpu as pltpu
from jax.sharding import PartitionSpec as P

MESH = pl.DeviceIdType.MESH
BF = jnp.bfloat16
F32 = jnp.float32
HD = 64
NT = 1000
NQ = 16
NS = 16
D = 3072
FR = 8
ROWS = 64
TOK = 1024
GROUP = 256
NC = 4
CW = D // NC
NK = 2
CK = D // NK
HR = ROWS // 2
QR = HR // 2
GR = GROUP // 2
FS = 384
HS = 192
M1 = 2 * D // 8
M2 = 4 * D // 8


def noise_level(times):
    angle = (times / NT + 0.008) / 1.008 * (math.pi / 2)
    cosine = jnp.cos(angle)
    return 0.05 + 0.94 * cosine * cosine


def dot_nt(a, b):
    return lax.dot_general(a, b, (((1,), (1,)), ((), ())), preferred_element_type=F32)


def dot(a, b):
    return jnp.dot(a, b, preferred_element_type=F32)


def lnorm(v):
    centre = v - jnp.mean(v, -1, keepdims=True)
    spread = jnp.mean(centre * centre, -1, keepdims=True)
    return centre * lax.rsqrt(spread + 1e-05)


def kernel(
    lev, lat, noise, patch_h, tw_h, ada_h, qkv_h, out_h, up_h, down_h, proj_h,
    both,
    patch, tw, ada, qkv, proj, wo, wu, wd,
    p1, p2, ra1, ra2, rb1, rb2, b1, b2, t1, t2, mod1, mod2,
    xs, xg, xet, acc_m, acc_s, abuf, mt, qt, kn, va, msend, mixt, mixa,
    res, own, s_o, s_r, s_l, p_r, p_l, rl, rr, ol, or_,
    nbuf, hacc, hid, fin, mv, cs, cr,
    lsem, ps, pr, ys, yr, zs, zr, fs, fr, mss, msr, xss, xrs,
    as_, ar, ss, sr, gs, gr, csem,
):
    q = lax.axis_index("queue")
    s = lax.axis_index("space")
    core = lax.rem(s, 2)
    x = lax.rem(s // 2, 4)
    y = s // 8

    def at(y_, x_, c_):
        return (y_ * 4 + x_) * 2 + c_

    mate = at(y, x, 1 - core)
    over = at(1 - y, x, core)
    q_flip = q + 1 - 2 * lax.rem(q, 2)
    right = at(y, lax.rem(x + 1, 4), core)
    left = at(y, lax.rem(x + 3, 4), core)
    q_next = lax.rem(q + 1, NQ)
    q_prev = lax.rem(q + NQ - 1, NQ)

    def local(i, src, dst):
        return pltpu.make_async_copy(src, dst, lsem.at[i])

    def remote(src, dst, ssem, rsem, sp, qq=None):
        return pltpu.make_async_remote_copy(
            src_ref=src, dst_ref=dst, send_sem=ssem, recv_sem=rsem,
            device_id=(q if qq is None else qq, sp), device_id_type=MESH,
        )

    c_tw = local(0, tw_h, tw)
    c_ada = local(1, ada_h, ada)
    c_patch = local(2, patch_h, patch)
    c_qkv = local(3, qkv_h, qkv)
    c_wo = local(4, out_h, wo.at[pl.ds(0, HS)])
    c_wu = local(5, up_h, wu.at[:, pl.ds(0, FS)])
    c_wd = local(6, down_h, wd.at[pl.ds(0, FS)])
    c_proj = local(7, proj_h, proj)
    for c in (c_tw, c_ada, c_patch, c_qkv):
        c.start()

    bar = pltpu.get_barrier_semaphore()

    group = ((mate, 1), (over, 2), (at(1 - y, x, 1 - core), 3))
    ring = ((right, 1), (at(y, lax.rem(x + 2, 4), core), 2), (left, 3))
    par = lax.rem(q // 2, 2)
    z_to = [lax.rem(q + NQ + 2 * (1 - 2 * par) * (1 - 2 * h), NQ) for h in range(2)]
    for dev in (
        [(q, o) for o, _ in group + ring]
        + [(q_flip, over), (q_next, s), (q_prev, s), (z_to[0], s), (z_to[1], s)]
    ):
        pl.semaphore_signal(bar, inc=1, device_id=dev, device_id_type=MESH)

    row = lax.broadcasted_iota(jnp.int32, (FR, 128), 0)
    now = jnp.zeros((FR, 128), F32)
    later = jnp.zeros((FR, 128), F32)
    for f in range(FR):
        t_now = lev[f, q].astype(F32)
        if f < FR - 1:
            t_later = lev[f + 1, q].astype(F32)
        else:
            t_later = lev[0, jnp.minimum(q + 1, NQ - 1)].astype(F32)
        now = jnp.where(row == f, t_now, now)
        later = jnp.where(row == f, t_later, later)
    a_now = noise_level(now)
    a_after = noise_level(later)
    a_after = jnp.where((row == FR - 1) & (q == NQ - 1), 1.0, a_after)
    keep = jnp.sqrt(a_after / a_now)
    mix = jnp.sqrt(1.0 - a_after) - jnp.sqrt(a_after * (1.0 - a_now) / a_now)

    half = D // 2
    lane = lax.broadcasted_iota(jnp.int32, (FR, half), 1).astype(F32)
    freqs = jnp.exp(-math.log(10000.0) * lane / half)
    angle = now[:, 0:1] * freqs
    c_tw.wait()
    pre = dot_nt(jnp.cos(angle).astype(BF), tw[:, 0:half]) + dot_nt(
        jnp.sin(angle).astype(BF), tw[:, half:D]
    )
    timing = (pre * jax.nn.sigmoid(pre)).astype(BF)
    c_ada.wait()
    for k in range(2):
        part = dot(timing, ada[k])
        for h in range(2):
            two = [part[:, (2 * h + i) * M1 : (2 * h + i + 1) * M1] for i in range(2)]
            p1[2 * k + h] = jnp.concatenate(two, 0).astype(BF)

    me4 = y * 2 + core
    pl.semaphore_wait(bar, 11)

    def slot_of(slot):
        return lax.rem(y + slot // 2, 2) * 2 + lax.rem(core + slot, 2)

    def group_sum(k, part, recv):
        ssem, rsem = mss.at[0, k], msr.at[0, k]
        return [
            remote(part.at[slot_of(i)], recv.at[i], ssem.at[i], rsem.at[i], o) for o, i in group
        ]

    def ring_sum(k, mine, recv):
        ssem, rsem = mss.at[1, k], msr.at[1, k]
        return [remote(mine, recv.at[i], ssem.at[i], rsem.at[i], o) for o, i in ring]

    def group_spread(k, tot):
        ssem, rsem = mss.at[2, k], msr.at[2, k]
        return [
            remote(tot.at[me4], tot.at[me4], ssem.at[i], rsem.at[i], o) for o, i in group
        ]

    x_near = [
        remote(xg.at[x, me4], xg.at[x, me4], xss.at[0, i], xrs.at[0, i], o) for o, i in group
    ]
    x_far = [remote(xg.at[x], xg.at[x], xss.at[1, i], xrs.at[1, i], o) for o, i in ring]

    def begin(copies):
        for c in copies:
            c.start()

    def arrive(copies):
        for c in copies:
            c.wait_recv()

    steps = []
    for k, (part, ra, mine, rb, tot) in enumerate(((p1, ra1, b1, rb1, t1), (p2, ra2, b2, rb2, t2))):
        steps.append((group_sum(k, part, ra), ring_sum(k, mine, rb), group_spread(k, tot)))

    def join(k):
        part, ra, mine = ((p1, ra1, b1), (p2, ra2, b2))[k]
        arrive(steps[k][0])
        acc = part[me4].astype(F32)
        for i in range(1, 4):
            acc += ra[i].astype(F32)
        mine[...] = acc.astype(BF)
        begin(steps[k][1])

    def close(k):
        mine, rb, tot = ((b1, rb1, t1), (b2, rb2, t2))[k]
        arrive(steps[k][1])
        acc = mine[...].astype(F32)
        for i in range(1, 4):
            acc += rb[i].astype(F32)
        tot[me4] = acc.astype(BF)
        begin(steps[k][2])

    def unpack(k):
        tot, mod, w = ((t1, mod1, M1), (t2, mod2, M2))[k]
        arrive(steps[k][2])
        for m in range(4):
            v = tot[m].astype(F32)
            mod[:, 2 * m * w : (2 * m + 1) * w] = v[0:FR]
            mod[:, (2 * m + 1) * w : (2 * m + 2) * w] = v[FR : 2 * FR]

    begin(steps[0][0])

    c_patch.wait()
    x_own = lat[...]
    res[...] = dot(x_own.astype(BF), patch[...])
    full = res[...]
    centre = full - jnp.mean(full, -1, keepdims=True)
    spread = jnp.mean(centre * centre, -1, keepdims=True)
    rstd = lax.rsqrt(spread + 1e-05)
    r_hi = rstd.astype(BF).astype(F32)
    r_mid = (rstd - r_hi).astype(BF).astype(F32)
    r_lo = rstd - r_hi - r_mid
    xs[...] = jnp.zeros_like(xs)
    xs[:, 0:HD] = x_own
    lane_x = lax.broadcasted_iota(jnp.int32, (ROWS, 128), 1)
    packed = xs[...]
    packed = jnp.where(lane_x == 64, r_hi, packed)
    packed = jnp.where(lane_x == 65, r_mid, packed)
    packed = jnp.where(lane_x == 66, r_lo, packed)
    xg[x, me4] = packed.astype(BF)
    begin(x_near)

    w_wo = remote(out_h, wo.at[pl.ds(HS, HS)], ps.at[0], pr.at[0], mate)
    w_wu = remote(up_h, wu.at[:, pl.ds(FS, FS)], ps.at[1], pr.at[1], mate)
    w_wd = remote(down_h, wd.at[pl.ds(FS, FS)], ps.at[2], pr.at[2], mate)

    y_pairs = []
    z_sends = []
    z_recvs = []
    f_copies = []

    def piece(i, source, target, forward_from, forward_to):
        mine = [2 * par + h for h in range(2)]
        theirs = [2 * (1 - par) + h for h in range(2)]
        y_pairs.append([
            remote(source(mine[h]), target(mine[h]), ys.at[i, h], yr.at[i, h], over, (q, q_flip)[h])
            for h in range(2)
        ])
        for lst, parts in ((z_sends, mine), (z_recvs, theirs)):
            lst.append([
                remote(target(parts[h]), target(parts[h]), zs.at[i, h], zr.at[i, h], s, z_to[h])
                for h in range(2)
            ])
        f_copies.append(remote(forward_from, forward_to, fs.at[i], fr.at[i], mate))

    def rows_of(base, part, size):
        return pl.ds(pl.multiple_of(base + part * size, 16), size)

    piece(
        0,
        lambda p: out_h.at[rows_of(0, p, HS // 4)],
        lambda p: wo.at[rows_of(2 * HS, p, HS // 4)],
        wo.at[pl.ds(2 * HS, HS)],
        wo.at[pl.ds(3 * HS, HS)],
    )
    for k in range(NC):
        piece(
            1 + k,
            lambda p, k=k: up_h.at[rows_of(k * CW, p, CW // 4)],
            lambda p, k=k: wu.at[rows_of(k * CW, p, CW // 4), pl.ds(2 * FS, FS)],
            wu.at[pl.ds(k * CW, CW), pl.ds(2 * FS, FS)],
            wu.at[pl.ds(k * CW, CW), pl.ds(3 * FS, FS)],
        )
    for k in range(NC):
        piece(
            1 + NC + k,
            lambda p, k=k: down_h.at[rows_of(0, p, FS // 4), pl.ds(k * CW, CW)],
            lambda p, k=k: wd.at[rows_of(2 * FS, p, FS // 4), pl.ds(k * CW, CW)],
            wd.at[pl.ds(2 * FS, FS), pl.ds(k * CW, CW)],
            wd.at[pl.ds(3 * FS, FS), pl.ds(k * CW, CW)],
        )

    def push(i):
        begin(y_pairs[i])

    def along(i):
        arrive(y_pairs[i])
        begin(z_sends[i])

    def forward(i):
        arrive(z_recvs[i])
        f_copies[i].start()

    c_wo.start()
    push(0)
    w_wo.start()
    c_proj.start()

    join(0)
    arrive(x_near)
    begin(x_far)
    for k in range(4):
        part = dot(timing, ada[2 + k])
        p2[k] = jnp.concatenate([part[:, 0:M2], part[:, M2 : 2 * M2]], 0).astype(BF)
    close(0)
    begin(steps[1][0])
    c_wu.start()
    w_wu.start()

    arrive(x_far)
    halves = [
        xg[b, m, h * HR : (h + 1) * HR] for h in range(2) for m in range(4) for b in range(4)
    ]
    xt = jnp.concatenate(halves, 0).astype(F32).T
    rstd_all = xt[64:65] + xt[65:66] + xt[66:67]
    frame = lax.rem(lax.broadcasted_iota(jnp.int32, (HD, TOK), 1), FR)
    xt = xt[0:HD]
    for f in range(FR):
        xet[f * HD : (f + 1) * HD, :] = jnp.where(frame == f, xt, 0.0).astype(BF)
    hot = (
        lax.rem(lax.broadcasted_iota(jnp.int32, (32, TOK), 1), FR)
        == lax.rem(lax.broadcasted_iota(jnp.int32, (32, TOK), 0), FR)
    ).astype(F32).astype(BF)

    along(0)
    acc_m[...] = jnp.zeros_like(acc_m)
    acc_s[...] = jnp.zeros_like(acc_s)
    hacc[...] = jnp.zeros_like(hacc)
    mean_w = jnp.mean(patch[...].astype(F32), -1, keepdims=True)
    c_qkv.wait()
    unpack(0)
    push(1)
    push(2)

    def fold_one(j, b):
        c = pl.ds(pl.multiple_of(j * CW, 128), CW)
        centred = patch[:, c].astype(F32) - mean_w
        gain = 1.0 + mod1[:, pl.ds(pl.multiple_of(D + j * CW, 128), CW)]
        for f in range(FR):
            abuf[b, f * HD : (f + 1) * HD, :] = (centred * gain[f : f + 1]).astype(BF)
        shift = mod1[:, c]
        hi = shift.astype(BF).astype(F32)
        both = jnp.concatenate([hi, shift - hi], 0).astype(BF)
        w = qkv[:, c]
        acc_m[...] += dot_nt(w, abuf[b])
        acc_s[...] += dot_nt(w, both)

    def fold(i, carry):
        fold_one(2 * i, 0)
        fold_one(2 * i + 1, 1)
        return carry

    join(1)
    lax.fori_loop(0, NC // 2, fold, 0)
    close(1)
    mt[...] = acc_m[...].astype(BF)
    s_hi = acc_s[...].astype(BF)
    s_lo = (acc_s[...] - s_hi.astype(F32)).astype(BF)
    s_all = jnp.concatenate([s_hi, s_lo], 1)

    def project(k):
        r = slice(k * HS, (k + 1) * HS)
        out = dot(mt[r, :], xet[...]) * rstd_all
        return (out + dot(s_all[r], hot)).reshape(3, HD, TOK)

    def head_norm(v):
        centre = v - jnp.mean(v, 1, keepdims=True)
        spread = jnp.mean(centre * centre, 1, keepdims=True)
        return centre * lax.rsqrt(spread + 1e-06)

    queries = head_norm(project(0)) * (HD**-0.5 / math.log(2.0))
    qt[...] = queries.astype(BF)
    keys = head_norm(project(1))
    for h in range(3):
        kn[h] = keys[h].T.astype(BF)
    values = project(2)
    for h in range(3):
        va[h, 0:HD, :] = values[h].astype(BF)
        va[h, HD : HD + 16, :] = jnp.ones((16, TOK), BF)

    def mix_copies(h):
        return [
            remote(msend.at[h, 0, 1 - core], mixt.at[h, 1], as_.at[h, 1], ar.at[h, 1], mate),
            remote(msend.at[h, 1, core], mixt.at[h, 2], as_.at[h, 2], ar.at[h, 2], over),
            remote(msend.at[h, 1, 1 - core], mixt.at[h, 3], as_.at[h, 3], ar.at[h, 3], group[2][0]),
        ]

    def attend(h):
        def part(i, carry):
            flip = 1 - i
            y_ = lax.rem(y + flip, 2)
            g = pl.ds(pl.multiple_of((h * 2 + y_) * GROUP, GROUP), GROUP)
            for n in range(3):
                asked = qt[n, :, g]
                o = jnp.zeros((HD + 16, GROUP), F32)
                for k in range(4):
                    some = slice(k * GROUP, (k + 1) * GROUP)
                    weights = jnp.exp2(dot(kn[n, some, :], asked)).astype(BF)
                    o += dot(va[n, :, some], weights)
                o = (o[0:HD] / o[HD : HD + 1]).astype(BF)
                for c in range(2):
                    msend[h, flip, c, n * HD : (n + 1) * HD, :] = o[:, c * GR : (c + 1) * GR]

            @pl.when(i == 0)
            def _():
                begin(mix_copies(h)[1:])

            return carry

        lax.fori_loop(0, 2, part, 0)
        begin(mix_copies(h)[:1])

    def turn(h):
        mixt[h, 0] = msend[h, 0, core]
        arrive(mix_copies(h))
        v = mixt[h].reshape(4 * HS, GR).astype(F32).T.astype(BF)
        for b in range(4):
            o = lax.rem(b - x + 4, 4)
            r = pl.ds(pl.multiple_of(o * HR, HR), HR)
            mixa[h, r, :] = v[b * HR : (b + 1) * HR]

    def chunk(j):
        return pl.ds(pl.multiple_of(j * CK, 128), CK)

    lo, hi16 = pl.ds(0, QR), pl.ds(QR, QR)

    def sends(p, h, j):
        c = chunk(j)

        def to(i, src, rows, dst, dst_rows, dev):
            return remote(
                src.at[h, rows, c], dst.at[p, h, dst_rows, c], ss.at[p, h, j, i], sr.at[p, h, j, i], dev
            )

        return [
            to(0, s_o, lo, ol, lo, right),
            to(1, s_o, hi16, or_, lo, left),
            to(2, s_r, hi16, rl, hi16, right),
            to(3, s_l, lo, rr, lo, left),
            to(4, s_r, lo, rl, lo, right),
            to(5, s_l, hi16, rr, hi16, left),
        ]

    def opened(p, h, term, late=()):
        def step(j, carry):
            @pl.when(j > 0)
            def _():
                arrive(late)

            c = chunk(j)
            v = term(h, c)
            m = sends(p, h, j)
            s_o[h, :, c] = v[2 * HR : 3 * HR].astype(BF)
            begin(m[0:2])
            s_r[h, QR:HR, c] = v[HR + QR : 2 * HR].astype(BF)
            s_l[h, 0:QR, c] = v[3 * HR : 3 * HR + QR].astype(BF)
            begin(m[2:4])
            p_r[h, :, c] = v[HR : HR + QR]
            p_l[h, :, c] = v[3 * HR + QR : 4 * HR]
            own[h, :, c] = v[0:HR]
            return carry

        lax.fori_loop(0, NK, step, 0)

    def passed(p, h):
        def step(j, carry):
            c = chunk(j)
            m = sends(p, h, j)
            m[0].wait_recv()
            s_r[h, 0:QR, c] = (p_r[h, :, c] + ol[p, h, :, c].astype(F32)).astype(BF)
            m[4].start()
            m[1].wait_recv()
            s_l[h, QR:HR, c] = (p_l[h, :, c] + or_[p, h, :, c].astype(F32)).astype(BF)
            m[5].start()
            return carry

        lax.fori_loop(0, NK, step, 0)

    def finish(p, h):
        def step(j, carry):
            arrive(sends(p, h, j)[2:])
            return carry

        lax.fori_loop(0, NK, step, 0)

    def sent(p, h):
        def step(j, carry):
            for c in sends(p, h, j):
                c.wait_send()
            return carry

        lax.fori_loop(0, NK, step, 0)

    def update(i, p, h, gate):
        r = pl.ds(pl.multiple_of(i * 16, 16), 16)
        rows = pl.ds(pl.multiple_of(h * HR + i * 16, 16), 16)
        summed = own[h, r, :] + rl[p, h, r, :].astype(F32) + rr[p, h, r, :].astype(F32)
        gated = mod2[:, gate * D : (gate + 1) * D] * summed.reshape(2, FR, D)
        return r, rows, res[rows, :].reshape(2, FR, D) + gated

    def second(h):
        def step(i, carry):
            r, rows, new = update(i, 0, h, 0)
            res[rows, :] = new.reshape(16, D)
            v = lnorm(new) * (1.0 + mod2[:, 2 * D : 3 * D]) + mod2[:, D : 2 * D]
            nbuf[h, r, :] = v.reshape(16, D).astype(BF)
            return carry

        lax.fori_loop(0, HR // 16, step, 0)

    def last(h):
        def step(i, carry):
            _, rows, new = update(i, 1, h, 3)
            fin[rows, :] = lnorm(new).reshape(16, D).astype(BF)
            return carry

        lax.fori_loop(0, HR // 16, step, 0)

    def gathers(h, j):
        c = chunk(j)

        def go(i, src, dst, dev):
            return remote(
                nbuf.at[h, pl.ds(src, QR), c], nbuf.at[h, pl.ds(dst, QR), c],
                gs.at[h, j, i], gr.at[h, j, i], dev,
            )

        return [
            go(0, 0, 3 * HR, right),
            go(1, QR, HR + QR, left),
            go(2, QR, 3 * HR + QR, right),
            go(3, 0, HR, left),
            go(4, 3 * HR, 2 * HR, right),
            go(5, HR + QR, 2 * HR + QR, left),
        ]

    def gather(h):
        def step(j, carry):
            begin(gathers(h, j)[:4])
            return carry

        lax.fori_loop(0, NK, step, 0)

    def relay(h, j):
        m = gathers(h, j)
        m[0].wait_recv()
        m[4].start()
        m[1].wait_recv()
        m[5].start()

    def widen(h, j):
        arrive(gathers(h, j)[2:])

        def step(n, carry):
            c = pl.ds(pl.multiple_of(n * 512, 512), 512)
            hacc[h, :, c] += dot(nbuf[h, :, j * CK : (j + 1) * CK], wu[j * CK : (j + 1) * CK, c])
            return carry

        lax.fori_loop(0, 3, step, 0)

    def activate(h):
        def step(i, carry):
            r = pl.ds(pl.multiple_of(i * 16, 16), 16)
            hid[h, r, :] = jax.nn.gelu(hacc[h, r, :], approximate=True).astype(BF)
            return carry

        lax.fori_loop(0, GR // 16, step, 0)

    def out_term(h, c):
        return dot(mixa[h], wo[:, c])

    def down_term(h, c):
        return dot(hid[h], wd[:, c])

    forward(0)
    attend(0)
    along(1)
    along(2)
    attend(1)
    push(3)
    push(4)
    turn(0)
    c_wo.wait()
    w_wo.wait_recv()
    f_copies[0].wait_recv()
    opened(0, 0, out_term)
    turn(1)
    for k in range(NC):
        push(1 + NC + k)
    c_wd.start()
    w_wd.start()
    passed(0, 0)
    opened(0, 1, out_term)
    unpack(1)
    forward(1)
    forward(2)
    along(3)
    along(4)
    passed(0, 1)
    finish(0, 0)
    second(0)
    gather(0)
    along(1 + NC)
    along(2 + NC)
    finish(0, 1)
    second(1)
    gather(1)
    forward(3)
    forward(4)
    for j in range(NK):
        relay(0, j)
    sent(0, 0)
    sent(0, 1)
    c_wu.wait()
    w_wu.wait_recv()
    arrive(f_copies[1:3])
    along(3 + NC)
    along(4 + NC)
    widen(0, 0)
    relay(1, 0)
    forward(1 + NC)
    forward(2 + NC)
    arrive(f_copies[3:5])
    widen(0, 1)
    relay(1, 1)
    activate(0)
    forward(3 + NC)
    forward(4 + NC)
    c_wd.wait()
    w_wd.wait_recv()
    arrive(f_copies[1 + NC : 3 + NC])
    opened(1, 0, down_term, f_copies[3 + NC :])
    widen(1, 0)
    widen(1, 1)
    activate(1)
    passed(1, 0)
    opened(1, 1, down_term)
    passed(1, 1)
    finish(1, 0)
    last(0)
    finish(1, 1)
    last(1)
    c_proj.wait()
    out = dot_nt(fin[...], proj[...])
    both[0] = out
    moved = keep[:, 0:HD] * lat[...].reshape(FR, FR, HD) + mix[:, 0:HD] * out.reshape(FR, FR, HD)
    mv[...] = jnp.zeros_like(mv)
    mv[:, 0:HD] = moved.reshape(ROWS, HD)
    cs[...] = mv[pl.ds(FR - 1, FR, stride=FR), :]
    carry_copy = remote(cs, cr, csem.at[0], csem.at[1], s, q_next)
    carry_copy.start()
    for f in range(1, FR):
        both[1, pl.ds(f, FR, stride=FR), :] = mv[pl.ds(f - 1, FR, stride=FR), :][:, 0:HD]

    for c in sum((list(t) for p in steps for t in p), x_near + x_far):
        c.wait_send()
    for h in range(2):
        for c in mix_copies(h):
            c.wait_send()
        sent(1, h)
    for c in (w_wo, w_wu, w_wd):
        c.wait_send()
    for pair in y_pairs + z_sends:
        for c in pair:
            c.wait_send()
    for c in f_copies:
        c.wait_send()

    for h in range(2):
        for j in range(NK):
            for c in gathers(h, j):
                c.wait_send()
    carry_copy.wait()
    both[1, pl.ds(0, FR, stride=FR), :] = jnp.where(q == 0, noise[...], cr[:, 0:HD])


def scratch():
    v = pltpu.VMEM
    dma = pltpu.SemaphoreType.DMA
    return [
        v((HD, D), BF), v((32, D), BF), v((6, 32, D), BF), v((3 * HS, D), BF), v((HD, D), BF),
        v((4 * HS, D), BF), v((D, 4 * FS), BF), v((4 * FS, D), BF),
        v((4, 16, M1), BF), v((4, 16, M2), BF), v((4, 16, M1), BF), v((4, 16, M2), BF),
        v((4, 16, M1), BF), v((4, 16, M2), BF), v((16, M1), BF), v((16, M2), BF),
        v((4, 16, M1), BF), v((4, 16, M2), BF), v((FR, 2 * D), F32), v((FR, 4 * D), F32),
        v((ROWS, 128), F32), v((4, 4, ROWS, 128), BF), v((FR * HD, TOK), BF),
        v((3 * HS, FR * HD), F32), v((3 * HS, 16), F32), v((2, FR * HD, CW), BF),
        v((3 * HS, FR * HD), BF),
        v((3, HD, TOK), BF), v((3, TOK, HD), BF), v((3, HD + 16, TOK), BF),
        v((2, 2, 2, HS, GR), BF), v((2, 4, HS, GR), BF), v((2, GR, 4 * HS), BF),
        v((ROWS, D), F32), v((2, HR, D), F32),
        v((2, HR, D), BF), v((2, HR, D), BF), v((2, HR, D), BF),
        v((2, QR, D), F32), v((2, QR, D), F32),
        v((2, 2, HR, D), BF), v((2, 2, HR, D), BF), v((2, 2, QR, D), BF), v((2, 2, QR, D), BF),
        v((2, GR, D), BF), v((2, GR, 4 * FS), F32), v((2, GR, 4 * FS), BF), v((ROWS, D), BF),
        v((ROWS, 128), F32), v((FR, 128), F32), v((FR, 128), F32),
        dma((8,)), dma((3,)), dma((3,)), dma((9, 2)), dma((9, 2)), dma((9, 2)), dma((9, 2)),
        dma((9,)), dma((9,)), dma((3, 2, 4)), dma((3, 2, 4)), dma((2, 4)), dma((2, 4)),
        dma((2, 4)), dma((2, 4)),
        dma((2, 2, NK, 6)), dma((2, 2, NK, 6)), dma((2, NK, 6)), dma((2, NK, 6)),
        dma((2,)),
    ]


def body(
    latents, fresh_noise, levels, patch_weight, time_weight, adaln_weight, qkv_weight,
    out_weight, up_weight, down_weight, proj_weight,
):
    vm = pl.BlockSpec(memory_space=pltpu.VMEM)
    hbm = pl.BlockSpec(memory_space=pl.ANY)
    both = pl.pallas_call(
        kernel,
        out_shape=jax.ShapeDtypeStruct((2, ROWS, HD), F32),
        in_specs=[pl.BlockSpec(memory_space=pltpu.SMEM), vm, vm] + [hbm] * 8,
        out_specs=vm,
        scratch_shapes=scratch(),
        compiler_params=pltpu.CompilerParams(
            collective_id=0, has_side_effects=True, vmem_limit_bytes=60 * 1024 * 1024
        ),
    )(
        levels.T,
        latents.reshape(ROWS, HD),
        fresh_noise.reshape(FR, HD),
        patch_weight,
        time_weight.T,
        jnp.transpose(adaln_weight, (1, 0, 2)),
        jnp.transpose(qkv_weight, (1, 2, 0)).reshape(3 * HS, D),
        out_weight,
        up_weight,
        down_weight,
        proj_weight.T,
    )
    return both[1].reshape(1, 8, FR, HD), both[0].reshape(1, 1, 8, FR, HD)


def solution(mesh):
    in_specs = (
        P("queue", "space", None, None),
        P(None, "space", None),
        P(),
        P(),
        P(None, "space"),
        P("space", None, None),
        P(None, None, "space"),
        P("space", None),
        P(None, "space"),
        P("space", None),
        P(),
    )
    out_specs = (P("queue", "space", None, None), P(None, "queue", "space", None, None))
    return jax.shard_map(body, mesh=mesh, in_specs=in_specs, out_specs=out_specs, check_vma=False)
```
